32 devices in a mesh: groups: 2 (over y), tm: 4 (over z), lat: 2 (over x), lon: 2 (over core).
Axes of the slice: x: 2, y: 2, z: 4, core: 2. Of those that a mesh axis runs over, the one named last changes fastest.
Arguments:
- prior_state: float32 [16, 8, 16, 256], P(('groups', 'tm'), None, 'lat', 'lon'), parts along dimension 0, may hold values from -6 to 6
- observed: float32 [16, 8, 16, 256], P(('groups', 'tm'), None, 'lat', 'lon'), parts along dimension 0, may hold values from -6 to 6
- obs_weight: float32 [16, 8, 16, 256], P(('groups', 'tm'), None, 'lat', 'lon'), parts along dimension 0, may hold values from 0 to 2
- noise_field: float32 [2, 16, 8, 16, 256], P(None, ('groups', 'tm'), None, 'lat', 'lon'), parts along dimension 1, may hold values from -6 to 6
- step_sizes: float32 [2], replicated, may hold values from 0.05 to 0.3
- lift_weight: float32 [96, 40], replicated, may hold values from -1 to 1
- conv_weights: bfloat16 [2, 9, 96, 96], replicated, may hold values from -0.21875 to 0.21875
- out_weight: bfloat16 [8, 96], replicated, may hold values from -0.625 to 0.625
Outputs:
- analysis: float32 [16, 8, 16, 256], P(('groups', 'tm'), None, 'lat', 'lon'), parts along dimension 0
The draws below stay inside these ranges and needn't reach their ends.
There are 2 independent parts, one for each index of `groups`. The reference program is written for one: setup_inputs(seed, part) draws one part's arguments, and reference() takes and returns one part's arrays. A program takes and returns all parts, laid end to end along the dimension named above; an argument that names none is the same for every part. Nothing has to cross between parts.
All inputs are finite; a program needn't handle non-finite values.
Results may differ from the reference program's by a relative error of at most 0.0012.
Values may be sent and summed in bfloat16 or wider, within the bound.
A program may use at most 64 MiB of HBM per device.

```python
import math
import jax
import jax.numpy as jnp
from jax import lax

C = 8
HIDDEN_SIZE = 96
STACK = 5
STEPS = 2
FRAMES = 8
LAT = 16
LON = 256


def block_scale(stream_key, dims, shards, least, high):
    factor_of, own = 1.0, jax.random.fold_in(stream_key, 6)
    for position, blocks in shards:
        draws = jnp.exp(jax.random.uniform(jax.random.fold_in(own, position), (blocks,), jnp.float32, least / len(shards), high / len(shards)))
        factor_of = factor_of * jnp.repeat(draws, dims[position] // blocks).reshape([-1 if axis == position else 1 for axis in range(len(dims))])
    return factor_of


def normal_values(stream_key, extent, spread, most, shards=(), kind=jnp.bfloat16):
    factor_of = block_scale(stream_key, extent, shards, -0.22, 0.18) if shards else 1.0
    array = jax.random.normal(stream_key, extent, jnp.float32) * spread * factor_of
    return jnp.minimum(jnp.maximum(array, -most), most).astype(kind)


def setup_inputs(seed: int = 0, part: int = 0) -> dict:
    seeds = jax.random.split(jax.random.key(seed), 9)
    part_splits = jax.random.split(jax.random.fold_in(seeds[8], part), 9)
    prior_state = normal_values(part_splits[0], (FRAMES, C, LAT, LON), 1.0, 6.0, ((0, 4), (2, 2), (3, 2)), jnp.float32)
    observed = normal_values(part_splits[1], (FRAMES, C, LAT, LON), 1.0, 6.0, ((0, 4), (2, 2), (3, 2)), jnp.float32)
    obs_weight = jnp.clip(2.0 * jax.random.uniform(part_splits[2], (FRAMES, C, LAT, LON), jnp.float32) ** block_scale(part_splits[2], (FRAMES, C, LAT, LON), ((0, 4), (2, 2), (3, 2)), -0.2, 0.2), 0.0, 2.0)
    noise_field = normal_values(part_splits[3], (STEPS, FRAMES, C, LAT, LON), 1.0, 6.0, ((1, 4), (3, 2), (4, 2)), jnp.float32)
    step_sizes = jnp.clip(jnp.exp(jax.random.uniform(seeds[4], (STEPS,), jnp.float32, math.log(0.05), math.log(0.3))), 0.05, 0.3)
    lift_weight = normal_values(seeds[5], (HIDDEN_SIZE, STACK * C), (STACK * C) ** -0.5, 1.0, (), jnp.float32)
    conv_weights = normal_values(seeds[6], (2, 9, HIDDEN_SIZE, HIDDEN_SIZE), (9 * HIDDEN_SIZE) ** -0.5, 0.21875)
    out_weight = normal_values(seeds[7], (C, HIDDEN_SIZE), HIDDEN_SIZE ** -0.5, 0.625)
    return dict(prior_state=prior_state, observed=observed, obs_weight=obs_weight, noise_field=noise_field, step_sizes=step_sizes, lift_weight=lift_weight, conv_weights=conv_weights, out_weight=out_weight)


def conv_layer(values, kernel):
    height = values.shape[1]
    width = values.shape[2]
    padded = jnp.pad(values, ((0, 0), (1, 1), (0, 0)))
    padded = jnp.concatenate([padded[:, :, -1:], padded, padded[:, :, :1]], axis=2)
    summed = jnp.zeros((kernel.shape[1], height, width), jnp.float32)
    for row_off in range(3):
        for col_off in range(3):
            tap = kernel[3 * row_off + col_off].astype(jnp.float32)
            part = padded[:, row_off:row_off + height, col_off:col_off + width].astype(jnp.float32)
            summed = summed + jnp.einsum('oi,ihw->ohw', tap, part)
    return summed

def score_all(current, lift_weight, conv_weights, out_weight):
    height = current.shape[2]
    width = current.shape[3]
    padded = jnp.pad(current, ((2, 2), (0, 0), (0, 0), (0, 0)))

    def frame_score(frame_index):
        window = lax.dynamic_slice_in_dim(padded, frame_index, 5, 0)
        stacked = window.reshape(-1, height, width)
        lifted = jnp.einsum('oc,chw->ohw', lift_weight, stacked, precision=lax.Precision.HIGHEST).astype(jnp.bfloat16)
        activated = jax.nn.silu(conv_layer(lifted, conv_weights[0])).astype(jnp.bfloat16)
        second = jax.nn.silu(conv_layer(activated, conv_weights[1]))
        merged = (lifted.astype(jnp.float32) + second).astype(jnp.bfloat16)
        return jnp.einsum('co,ohw->chw', out_weight.astype(jnp.float32), merged.astype(jnp.float32))
    return lax.map(frame_score, jnp.arange(current.shape[0], dtype=jnp.int32))

def reference(prior_state, observed, obs_weight, noise_field, step_sizes, lift_weight, conv_weights, out_weight):
    current = prior_state
    for update in range(noise_field.shape[0]):
        step_size = step_sizes[update]
        score = score_all(current, lift_weight, conv_weights, out_weight)
        current = current + step_size * (score + obs_weight * (observed - current)) + jnp.sqrt(2.0 * step_size) * noise_field[update]
    return current
```

```python
import functools

import jax
import jax.numpy as jnp
from jax import lax
from jax.experimental import pallas as pl
from jax.experimental.pallas import tpu as pltpu
from jax.sharding import PartitionSpec as P

F32 = jnp.float32
BF16 = jnp.bfloat16
LANES = 128
GUARD = 8


def silu(value):
    half = 0.5 * value
    return half + half * jnp.tanh(half)


def transposed(matrix):
    return jnp.transpose(matrix.astype(F32))


def kernel(
    dims,
    steps_ref,
    prior_hbm,
    observed_hbm,
    obs_weight_hbm,
    noise_hbm,
    lift_hbm,
    conv_hbm,
    out_weight_hbm,
    result_ref,
    prior,
    observed,
    obs_weight,
    noise,
    lift_in,
    conv_in,
    out_in,
    load_sem,
    send_sem,
    recv_sem,
    state,
    main,
    edge_out,
    edge_in,
    lift_f32,
    lift_w,
    conv_w,
    out_f32,
    out_w,
    lifted,
    lifted_cols,
    activated,
    activated_cols,
):
    frames, chans, rows, cols, hidden, updates, margin = dims
    tile = frames * chans
    group = cols // rows
    span = rows + 2 * margin
    wide = cols + 2 * GUARD
    t, t_size = lax.axis_index("tm"), lax.axis_size("tm")
    l, l_size = lax.axis_index("lat"), lax.axis_size("lat")
    other = lax.rem(lax.axis_index("lon") + 1, lax.axis_size("lon"))

    loads = [
        pltpu.make_async_copy(source, target, load_sem.at[index])
        for index, (source, target) in enumerate(
            (
                (prior_hbm, prior),
                (conv_hbm, conv_in),
                (lift_hbm, lift_in),
                (out_weight_hbm, out_in),
                (observed_hbm, observed),
                (obs_weight_hbm, obs_weight),
                (noise_hbm, noise),
            )
        )
    ]
    for load in loads:
        load.start()

    main[...] = jnp.zeros_like(main)
    edge_in[...] = jnp.zeros_like(edge_in)

    around = [
        (dt, dl, do)
        for dt in (-1, 0, 1)
        for dl in (-1, 0, 1)
        for do in (0, 1)
        if (dt, dl, do) != (0, 0, 0)
    ]

    def exists(dt, dl):
        return (t + dt >= 0) & (t + dt < t_size) & (l + dl >= 0) & (l + dl < l_size)

    def target(dt, dl, do):
        own = lax.axis_index("lon")
        return {"tm": t + dt, "lat": l + dl, "lon": other if do else own}

    barrier = pltpu.get_barrier_semaphore()
    for dt, dl, do in around:

        @pl.when(exists(dt, dl))
        def _():
            pl.semaphore_signal(
                barrier, inc=1, device_id=target(dt, dl, do), device_id_type=pl.DeviceIdType.MESH
            )

    def one(flag):
        return flag.astype(jnp.int32)

    t_count = 1 + one(t > 0) + one(t < t_size - 1)
    l_count = 1 + one(l > 0) + one(l < l_size - 1)

    def message(u, dt, dl, do):
        slot, kind = 1 - dt, 1 - dl
        if do:
            source, place = edge_out.at[u], edge_in.at[u, slot, kind]
        elif dl == 0:
            source = main.at[u, 1, pl.ds(margin, rows)]
            place = main.at[u, slot, pl.ds(margin, rows)]
        elif dl == 1:
            source = main.at[u, 1, pl.ds(rows, margin)]
            place = main.at[u, slot, pl.ds(0, margin)]
        else:
            source = main.at[u, 1, pl.ds(margin, margin)]
            place = main.at[u, slot, pl.ds(margin + rows, margin)]
        where = (slot * 3 + kind) * 2 + do
        return pltpu.make_async_remote_copy(
            src_ref=source,
            dst_ref=place,
            send_sem=send_sem.at[u, where],
            recv_sem=recv_sem.at[u, where],
            device_id=target(dt, dl, do),
            device_id_type=pl.DeviceIdType.MESH,
        )

    lane_group = lax.broadcasted_iota(jnp.int32, (tile, cols), 1) // group

    def send_all(u):
        edge = jnp.zeros((tile, cols), F32)
        for row in range(rows):
            value = state[row]
            main[u, 1, margin + row] = value.astype(BF16)
            turned = pltpu.roll(value, (group * row + group // 2) % cols, 1)
            edge = jnp.where(lane_group == row, turned, edge)
        edge_out[u] = edge.astype(BF16)
        if u == 0:
            pl.semaphore_wait(barrier, t_count * l_count * 2 - 1)
        for dt, dl, do in around:

            @pl.when(exists(dt, dl))
            def _():
                message(u, dt, dl, do).start()

    def receive_all(u):
        for dt, dl, do in around:

            @pl.when(exists(-dt, -dl))
            def _():
                message(u, dt, dl, do).wait_recv()

    def strided(frame, row):
        return pl.ds(frame * chans * rows + row, chans, stride=rows)

    loads[0].wait()
    for row in range(rows):
        state[row] = jnp.concatenate(
            [prior[strided(frame, row), :] for frame in range(frames)], axis=0
        )
    send_all(0)

    lift_f32[...] = jnp.zeros_like(lift_f32)
    conv_w[...] = jnp.zeros_like(conv_w)
    out_f32[...] = jnp.zeros_like(out_f32)
    lifted[...] = jnp.zeros_like(lifted)
    for load in loads[1:4]:
        load.wait()
    depth = lift_in.shape[1]
    pile = 3 * tile
    turned = transposed(lift_in[...])
    high = turned.astype(BF16).astype(F32)
    low = turned - high
    for part, value in enumerate((high, low)):
        for frame in range(frames):
            lift_f32[pl.ds(part * pile + frame * chans, depth), pl.ds(frame * LANES, hidden)] = value
    lift_w[...] = lift_f32[...].astype(BF16)
    for layer in range(2):
        for a in range(3):
            for b in range(3):
                tap = transposed(conv_in[layer, 3 * a + b]).astype(BF16)
                for q in range(2):
                    conv_w[
                        layer, pl.ds(((a + q) * 3 + b) * LANES, hidden), pl.ds(q * LANES, hidden)
                    ] = tap
    for q in range(2):
        out_f32[pl.ds(q * chans, chans), pl.ds(q * LANES, hidden)] = out_in[...].astype(F32)
    out_w[...] = out_f32[...].astype(BF16)
    for load in loads[4:]:
        load.wait()

    def lift(values):
        stacked = jnp.concatenate(values + values, axis=0)
        result = lax.dot_general(
            stacked, lift_w[...], (((0,), (0,)), ((), ())), preferred_element_type=F32
        )
        return result.astype(BF16).astype(F32)

    for u in range(updates):
        receive_all(u)

        for row in range(span):
            lifted[row, pl.ds(GUARD, cols)] = lift([main[u, slot, row] for slot in range(3)])
        own_edge = lift([edge_in[u, slot, 1] for slot in range(3)])
        far_edge = lift(
            [
                jnp.where(
                    lane_group < rows // 2,
                    edge_in[u, slot, 2].astype(F32),
                    edge_in[u, slot, 0].astype(F32),
                ).astype(BF16)
                for slot in range(3)
            ]
        )
        for row in range(span):
            if row < margin:
                start, edge = group * (rows - margin + row), far_edge
            elif row < margin + rows:
                start, edge = group * (row - margin), own_edge
            else:
                start, edge = group * (row - margin - rows), far_edge
            middle = start + group // 2
            lifted[row, pl.ds(0, GUARD)] = edge[middle - GUARD : middle]
            lifted[row, pl.ds(GUARD + cols, GUARD)] = edge[middle : middle + GUARD]
        for row in range(span):
            for b in range(3):
                lifted_cols[b, row] = lifted[row, pl.ds(GUARD - 2 + b, wide)].astype(BF16)

        top = jnp.where(l == 0, 0.0, 1.0).astype(F32)
        bottom = jnp.where(l == l_size - 1, 0.0, 1.0).astype(F32)
        pairs = rows // 2 + 1
        for pair in range(pairs):
            for frame in range(frames):
                part = pl.ds(frame * LANES, LANES)
                window = jnp.concatenate(
                    [lifted_cols[b, 2 * pair + r, :, part] for r in range(4) for b in range(3)],
                    axis=1,
                )
                result = silu(jnp.dot(window, conv_w[0], preferred_element_type=F32))
                for q in range(2):
                    value = result[:, q * LANES : (q + 1) * LANES]
                    if pair == 0 and q == 0:
                        value = value * top
                    if pair == pairs - 1 and q == 1:
                        value = value * bottom
                    activated[frame, 2 * pair + q] = value
        for frame in range(frames):
            for row in range(rows + 2):
                for b in range(3):
                    activated_cols[b, frame, row] = activated[frame, row, pl.ds(b, cols)].astype(BF16)

        step = jnp.full((chans, cols), steps_ref[u], F32)
        spread = jnp.sqrt(2.0 * step)
        for pair in range(rows // 2):
            for frame in range(frames):
                part = pl.ds(frame * LANES, LANES)
                window = jnp.concatenate(
                    [activated_cols[b, frame, 2 * pair + r] for r in range(4) for b in range(3)],
                    axis=1,
                )
                second = silu(jnp.dot(window, conv_w[1], preferred_element_type=F32))
                base = jnp.concatenate(
                    [lifted[margin + 2 * pair + q, pl.ds(GUARD, cols), part] for q in range(2)],
                    axis=1,
                )
                merged = (base + second).astype(BF16)
                score = lax.dot_general(
                    out_w[...], merged, (((1,), (1,)), ((), ())), preferred_element_type=F32
                )
                for q in range(2):
                    row = 2 * pair + q
                    own = pl.ds(frame * chans, chans)
                    where = strided(frame, row)
                    current = state[row, own]
                    pull = obs_weight[where, :] * (observed[where, :] - current)
                    fresh = (
                        current
                        + step * (score[q * chans : (q + 1) * chans] + pull)
                        + spread * noise[u, where, :]
                    )
                    if u == updates - 1:
                        result_ref[where, :] = fresh
                    else:
                        state[row, own] = fresh
        if u < updates - 1:
            send_all(u + 1)

    for u in range(updates):
        for dt, dl, do in around:

            @pl.when(exists(dt, dl))
            def _():
                message(u, dt, dl, do).wait_send()


def per_device(
    prior_state, observed, obs_weight, noise_field, step_sizes, lift_weight, conv_weights, out_weight
):
    frames, chans, rows, cols = prior_state.shape
    hidden, depth = lift_weight.shape
    updates = noise_field.shape[0]
    margin = 2
    tile = frames * chans
    span = rows + 2 * margin
    wide = cols + 2 * GUARD
    flat = (tile * rows, cols)
    dims = (frames, chans, rows, cols, hidden, updates, margin)
    vmem = pltpu.VMEM
    result = pl.pallas_call(
        functools.partial(kernel, dims),
        out_shape=jax.ShapeDtypeStruct(flat, F32),
        in_specs=[pl.BlockSpec(memory_space=pltpu.SMEM)] + [pl.BlockSpec(memory_space=pl.ANY)] * 7,
        out_specs=pl.BlockSpec(memory_space=pltpu.VMEM),
        scratch_shapes=[
            vmem(flat, F32),
            vmem(flat, F32),
            vmem(flat, F32),
            vmem((updates, *flat), F32),
            vmem(lift_weight.shape, F32),
            vmem(conv_weights.shape, BF16),
            vmem(out_weight.shape, BF16),
            pltpu.SemaphoreType.DMA((7,)),
            pltpu.SemaphoreType.DMA((updates, 18)),
            pltpu.SemaphoreType.DMA((updates, 18)),
            vmem((rows, tile, cols), F32),
            vmem((updates, 3, span, tile, cols), BF16),
            vmem((updates, tile, cols), BF16),
            vmem((updates, 3, 3, tile, cols), BF16),
            vmem((6 * tile, frames * LANES), F32),
            vmem((6 * tile, frames * LANES), BF16),
            vmem((2, 12 * LANES, 2 * LANES), BF16),
            vmem((2 * chans, 2 * LANES), F32),
            vmem((2 * chans, 2 * LANES), BF16),
            vmem((span, wide + GUARD, frames * LANES), F32),
            vmem((3, span, wide, frames * LANES), BF16),
            vmem((frames, rows + 2, wide, LANES), F32),
            vmem((3, frames, rows + 2, cols, LANES), BF16),
        ],
        compiler_params=pltpu.CompilerParams(
            collective_id=0, has_side_effects=True, vmem_limit_bytes=40 * 1024 * 1024
        ),
        cost_estimate=pl.CostEstimate(
            flops=4 * updates * tile * rows * cols * hidden * 9 * hidden // chans,
            bytes_accessed=1 << 20,
            transcendentals=0,
        ),
    )(
        step_sizes,
        prior_state.reshape(flat),
        observed.reshape(flat),
        obs_weight.reshape(flat),
        noise_field.reshape(updates, *flat),
        lift_weight,
        conv_weights,
        out_weight,
    )
    return result.reshape(prior_state.shape)


def solution(mesh):
    placed = (
        P(("groups", "tm"), None, "lat", "lon"),
        P(("groups", "tm"), None, "lat", "lon"),
        P(("groups", "tm"), None, "lat", "lon"),
        P(None, ("groups", "tm"), None, "lat", "lon"),
        P(),
        P(),
        P(),
        P(),
    )
    return jax.shard_map(
        per_device,
        mesh=mesh,
        in_specs=placed,
        out_specs=P(("groups", "tm"), None, "lat", "lon"),
        check_vma=False,
    )
```

```python
import functools

import jax
import jax.numpy as jnp
from jax import lax
from jax.experimental import pallas as pl
from jax.experimental.pallas import tpu as pltpu
from jax.sharding import PartitionSpec as P

F32 = jnp.float32
BF16 = jnp.bfloat16
LANES = 128
GUARD = 8


def silu(value):
    half = 0.5 * value
    return half + half * jnp.tanh(half)


def transposed(matrix):
    return jnp.transpose(matrix.astype(F32))


def kernel(
    dims,
    steps_ref,
    prior_hbm,
    observed_hbm,
    obs_weight_hbm,
    noise_hbm,
    lift_hbm,
    conv_hbm,
    out_weight_hbm,
    result_ref,
    prior,
    observed,
    obs_weight,
    noise,
    lift_in,
    conv_in,
    out_in,
    load_sem,
    send_sem,
    recv_sem,
    state,
    main,
    edge_out,
    edge_in,
    lift_f32,
    lift_w,
    conv_w,
    out_f32,
    out_w,
    lifted,
    lifted_cols,
    activated,
    activated_cols,
):
    frames, chans, rows, cols, hidden, updates, margin = dims
    tile = frames * chans
    group = cols // rows
    span = rows + 2 * margin
    wide = cols + 2 * GUARD
    t, t_size = lax.axis_index("tm"), lax.axis_size("tm")
    l, l_size = lax.axis_index("lat"), lax.axis_size("lat")
    other = lax.rem(lax.axis_index("lon") + 1, lax.axis_size("lon"))

    loads = [
        pltpu.make_async_copy(source, target, load_sem.at[index])
        for index, (source, target) in enumerate(
            (
                (prior_hbm, prior),
                (conv_hbm, conv_in),
                (lift_hbm, lift_in),
                (out_weight_hbm, out_in),
                (observed_hbm, observed),
                (obs_weight_hbm, obs_weight),
                (noise_hbm, noise),
            )
        )
    ]
    for load in loads:
        load.start()

    main[...] = jnp.zeros_like(main)
    edge_in[...] = jnp.zeros_like(edge_in)

    around = [
        (dt, dl, do)
        for dt in (-1, 0, 1)
        for dl in (-1, 0, 1)
        for do in (0, 1)
        if (dt, dl, do) != (0, 0, 0)
    ]

    def exists(dt, dl):
        return (t + dt >= 0) & (t + dt < t_size) & (l + dl >= 0) & (l + dl < l_size)

    def target(dt, dl, do):
        own = lax.axis_index("lon")
        return {"tm": t + dt, "lat": l + dl, "lon": other if do else own}

    barrier = pltpu.get_barrier_semaphore()
    for dt, dl, do in around:

        @pl.when(exists(dt, dl))
        def _():
            pl.semaphore_signal(
                barrier, inc=1, device_id=target(dt, dl, do), device_id_type=pl.DeviceIdType.MESH
            )

    def one(flag):
        return flag.astype(jnp.int32)

    t_count = 1 + one(t > 0) + one(t < t_size - 1)
    l_count = 1 + one(l > 0) + one(l < l_size - 1)

    def message(u, dt, dl, do, chunk=0):
        slot, kind = 1 - dt, 1 - dl
        first, count = (margin * chunk, margin) if u else (0, rows)
        if do:
            source, place = edge_out.at[u], edge_in.at[u, slot, kind]
        elif dl == 0:
            source = main.at[u, 1, pl.ds(margin + first, count)]
            place = main.at[u, slot, pl.ds(margin + first, count)]
        elif dl == 1:
            source = main.at[u, 1, pl.ds(rows, margin)]
            place = main.at[u, slot, pl.ds(0, margin)]
        else:
            source = main.at[u, 1, pl.ds(margin, margin)]
            place = main.at[u, slot, pl.ds(margin + rows, margin)]
        where = ((slot * 3 + kind) * 2 + do) * (rows // margin) + chunk
        return pltpu.make_async_remote_copy(
            src_ref=source,
            dst_ref=place,
            send_sem=send_sem.at[u, where],
            recv_sem=recv_sem.at[u, where],
            device_id=target(dt, dl, do),
            device_id_type=pl.DeviceIdType.MESH,
        )

    lane_group = lax.broadcasted_iota(jnp.int32, (tile, cols), 1) // group

    def halves(value):
        high = value.astype(BF16)
        return jnp.concatenate([high, (value - high.astype(F32)).astype(BF16)], axis=0)

    def send(u, dt, dl, do, chunk=0):
        @pl.when(exists(dt, dl))
        def _():
            message(u, dt, dl, do, chunk).start()

    def chunks_of(u, dl, do):
        return range(rows // margin) if u and dl == 0 and not do else range(1)

    def keep(u, row, value):
        state[row] = value
        main[u, 1, margin + row] = halves(value)

    def send_chunk(u, chunk):
        for dt in (-1, 1):
            send(u, dt, 0, 0, chunk)
        if chunk == 0:
            for dt in (-1, 0, 1):
                send(u, dt, -1, 0)
        if chunk == rows // margin - 1:
            for dt in (-1, 0, 1):
                send(u, dt, 1, 0)

    def send_edges(u):
        edge = jnp.zeros((tile, cols), F32)
        for row in range(rows):
            turned = pltpu.roll(state[row], (group * row + group // 2) % cols, 1)
            edge = jnp.where(lane_group == row, turned, edge)
        edge_out[u] = halves(edge)
        for dt in (-1, 0, 1):
            for dl in (-1, 0, 1):
                send(u, dt, dl, 1)

    def receive_all(u):
        for dt, dl, do in around:

            @pl.when(exists(-dt, -dl))
            def _():
                for chunk in chunks_of(u, dl, do):
                    message(u, dt, dl, do, chunk).wait_recv()

    def strided(frame, row):
        return pl.ds(frame * chans * rows + row, chans, stride=rows)

    loads[0].wait()
    for row in range(rows):
        keep(
            0,
            row,
            jnp.concatenate([prior[strided(frame, row), :] for frame in range(frames)], axis=0),
        )
    pl.semaphore_wait(barrier, t_count * l_count * 2 - 1)
    for dt in (-1, 1):
        send(0, dt, 0, 0)
    for dt in (-1, 0, 1):
        for dl in (-1, 1):
            send(0, dt, dl, 0)
    send_edges(0)

    lift_f32[...] = jnp.zeros_like(lift_f32)
    conv_w[...] = jnp.zeros_like(conv_w)
    out_f32[...] = jnp.zeros_like(out_f32)
    lifted[...] = jnp.zeros_like(lifted)
    for load in loads[1:4]:
        load.wait()
    depth = lift_in.shape[0]
    turned = lift_in[...]
    high = turned.astype(BF16).astype(F32)
    low = turned - high
    for frame in range(frames):
        part = pl.ds(frame * LANES, hidden)
        for item in range(depth // chans):
            source = slice(item * chans, (item + 1) * chans)
            slot, place = divmod((item + frame) * chans, tile)
            lift_f32[pl.ds(slot * 2 * tile + place, chans), part] = high[source]
            lift_f32[pl.ds(slot * 2 * tile + tile + place, chans), part] = high[source]
            lift_f32[pl.ds(6 * tile + slot * tile + place, chans), part] = low[source]
    lift_w[...] = lift_f32[...].astype(BF16)
    for layer in range(2):
        for a in range(3):
            for b in range(3):
                tap = transposed(conv_in[layer, 3 * a + b]).astype(BF16)
                for q in range(2):
                    conv_w[
                        layer, pl.ds(((a + q) * 3 + b) * LANES, hidden), pl.ds(q * LANES, hidden)
                    ] = tap
    for q in range(2):
        out_f32[pl.ds(q * chans, chans), pl.ds(q * LANES, hidden)] = out_in[...].astype(F32)
    out_w[...] = out_f32[...].astype(BF16)
    for load in loads[4:]:
        load.wait()

    lane_kind = lane_group < rows // 2

    for u in range(updates):
        receive_all(u)

        def far(slot):
            low_rows = edge_in[u, slot, 2].astype(F32)
            high_rows = edge_in[u, slot, 0].astype(F32)
            kind = jnp.concatenate([lane_kind, lane_kind], axis=0)
            return jnp.where(kind, low_rows, high_rows).astype(BF16)

        sides = [main[u, slot] for slot in range(3)]
        blocks = [[sides[slot][row] for slot in range(3)] for row in range(span)]
        blocks.append([edge_in[u, slot, 1] for slot in range(3)])
        blocks.append([far(slot) for slot in range(3)])
        stacked = jnp.concatenate(
            [jnp.concatenate(block + [part[:tile] for part in block], axis=0) for block in blocks],
            axis=1,
        )
        result = lax.dot_general(
            stacked, lift_w[...], (((0,), (0,)), ((), ())), preferred_element_type=F32
        )
        result = result.astype(BF16).astype(F32)
        own_edge = result[span * cols : (span + 1) * cols]
        far_edge = result[(span + 1) * cols :]
        for row in range(span):
            if row < margin:
                start, edge = group * (rows - margin + row), far_edge
            elif row < margin + rows:
                start, edge = group * (row - margin), own_edge
            else:
                start, edge = group * (row - margin - rows), far_edge
            middle = start + group // 2
            lifted[row, pl.ds(GUARD, cols)] = result[row * cols : (row + 1) * cols]
            lifted[row, pl.ds(0, GUARD)] = edge[middle - GUARD : middle]
            lifted[row, pl.ds(GUARD + cols, GUARD)] = edge[middle : middle + GUARD]
        for row in range(span):
            for b in range(3):
                for frame in range(frames):
                    part = pl.ds(frame * LANES, LANES)
                    lifted_cols[b, row % 2, row // 2, frame] = lifted[
                        row, pl.ds(GUARD - 2 + b, wide), part
                    ].astype(BF16)

        top = jnp.where(l == 0, 0.0, 1.0).astype(F32)
        bottom = jnp.where(l == l_size - 1, 0.0, 1.0).astype(F32)
        pairs = rows // 2 + 1
        for pair in range(pairs):
            window = jnp.concatenate(
                [
                    lifted_cols[b, r % 2, pair + r // 2].reshape(frames * wide, LANES)
                    for r in range(4)
                    for b in range(3)
                ],
                axis=1,
            )
            result = silu(jnp.dot(window, conv_w[0], preferred_element_type=F32))
            for frame in range(frames):
                for q in range(2):
                    value = result[frame * wide : (frame + 1) * wide, q * LANES : (q + 1) * LANES]
                    if pair == 0 and q == 0:
                        value = value * top
                    if pair == pairs - 1 and q == 1:
                        value = value * bottom
                    activated[frame, 2 * pair + q] = value
                    for b in range(3):
                        activated_cols[b, q, pair, frame] = activated[
                            frame, 2 * pair + q, pl.ds(b, cols)
                        ].astype(BF16)

        step = jnp.full((chans, cols), steps_ref[u], F32)
        spread = jnp.sqrt(2.0 * step)
        for pair in range(rows // 2):
            window = jnp.concatenate(
                [
                    activated_cols[b, r % 2, pair + r // 2].reshape(frames * cols, LANES)
                    for r in range(4)
                    for b in range(3)
                ],
                axis=1,
            )
            second = silu(jnp.dot(window, conv_w[1], preferred_element_type=F32))
            base = jnp.concatenate(
                [
                    jnp.concatenate(
                        [
                            lifted[
                                margin + 2 * pair + q, pl.ds(GUARD, cols), pl.ds(frame * LANES, LANES)
                            ]
                            for q in range(2)
                        ],
                        axis=1,
                    )
                    for frame in range(frames)
                ],
                axis=0,
            )
            merged = (base + second).astype(BF16)
            score = lax.dot_general(
                out_w[...], merged, (((1,), (1,)), ((), ())), preferred_element_type=F32
            )
            for q in range(2):
                row = 2 * pair + q
                fresh = []
                for frame in range(frames):
                    where = strided(frame, row)
                    current = state[row, pl.ds(frame * chans, chans)]
                    drift = score[q * chans : (q + 1) * chans, frame * cols : (frame + 1) * cols]
                    pull = obs_weight[where, :] * (observed[where, :] - current)
                    value = current + step * (drift + pull) + spread * noise[u, where, :]
                    fresh.append(value)
                    if u == updates - 1:
                        result_ref[where, :] = value
                if u < updates - 1:
                    keep(u + 1, row, jnp.concatenate(fresh, axis=0))
            if u < updates - 1:
                send_chunk(u + 1, pair)
        if u < updates - 1:
            send_edges(u + 1)

    for u in range(updates):
        for dt, dl, do in around:

            @pl.when(exists(dt, dl))
            def _():
                for chunk in chunks_of(u, dl, do):
                    message(u, dt, dl, do, chunk).wait_send()


def per_device(
    prior_state, observed, obs_weight, noise_field, step_sizes, lift_weight, conv_weights, out_weight
):
    frames, chans, rows, cols = prior_state.shape
    hidden, depth = lift_weight.shape
    updates = noise_field.shape[0]
    margin = 2
    tile = frames * chans
    span = rows + 2 * margin
    wide = cols + 2 * GUARD
    flat = (tile * rows, cols)
    dims = (frames, chans, rows, cols, hidden, updates, margin)
    vmem = pltpu.VMEM
    result = pl.pallas_call(
        functools.partial(kernel, dims),
        out_shape=jax.ShapeDtypeStruct(flat, F32),
        in_specs=[pl.BlockSpec(memory_space=pltpu.SMEM)] + [pl.BlockSpec(memory_space=pl.ANY)] * 7,
        out_specs=pl.BlockSpec(memory_space=pltpu.VMEM),
        scratch_shapes=[
            vmem(flat, F32),
            vmem(flat, F32),
            vmem(flat, F32),
            vmem((updates, *flat), F32),
            vmem((depth, hidden), F32),
            vmem(conv_weights.shape, BF16),
            vmem(out_weight.shape, BF16),
            pltpu.SemaphoreType.DMA((7,)),
            pltpu.SemaphoreType.DMA((updates, 18 * (rows // margin))),
            pltpu.SemaphoreType.DMA((updates, 18 * (rows // margin))),
            vmem((rows, tile, cols), F32),
            vmem((updates, 3, span, 2 * tile, cols), BF16),
            vmem((updates, 2 * tile, cols), BF16),
            vmem((updates, 3, 3, 2 * tile, cols), BF16),
            vmem((9 * tile, frames * LANES), F32),
            vmem((9 * tile, frames * LANES), BF16),
            vmem((2, 12 * LANES, 2 * LANES), BF16),
            vmem((2 * chans, 2 * LANES), F32),
            vmem((2 * chans, 2 * LANES), BF16),
            vmem((span, wide + GUARD, frames * LANES), F32),
            vmem((3, 2, span // 2, frames, wide, LANES), BF16),
            vmem((frames, rows + 2, wide, LANES), F32),
            vmem((3, 2, rows // 2 + 1, frames, cols, LANES), BF16),
        ],
        compiler_params=pltpu.CompilerParams(
            collective_id=0, has_side_effects=True, vmem_limit_bytes=60 * 1024 * 1024
        ),
        cost_estimate=pl.CostEstimate(
            flops=4 * updates * tile * rows * cols * hidden * 9 * hidden // chans,
            bytes_accessed=1 << 20,
            transcendentals=0,
        ),
    )(
        step_sizes,
        prior_state.reshape(flat),
        observed.reshape(flat),
        obs_weight.reshape(flat),
        noise_field.reshape(updates, *flat),
        lift_weight.T,
        conv_weights,
        out_weight,
    )
    return result.reshape(prior_state.shape)


def solution(mesh):
    placed = (
        P(("groups", "tm"), None, "lat", "lon"),
        P(("groups", "tm"), None, "lat", "lon"),
        P(("groups", "tm"), None, "lat", "lon"),
        P(None, ("groups", "tm"), None, "lat", "lon"),
        P(),
        P(),
        P(),
        P(),
    )
    return jax.shard_map(
        per_device,
        mesh=mesh,
        in_specs=placed,
        out_specs=P(("groups", "tm"), None, "lat", "lon"),
        check_vma=False,
    )
```

```python
import functools

import jax
import jax.numpy as jnp
from jax import lax
from jax.experimental import pallas as pl
from jax.experimental.pallas import tpu as pltpu
from jax.sharding import PartitionSpec as P

F32 = jnp.float32
BF16 = jnp.bfloat16
LANES = 128
GUARD = 8


def silu(value):
    half = 0.5 * value
    return half + half * jnp.tanh(half)


def transposed(matrix):
    return jnp.transpose(matrix.astype(F32))


def kernel(
    dims,
    steps_ref,
    prior_hbm,
    observed_hbm,
    obs_weight_hbm,
    noise_hbm,
    lift_hbm,
    conv_hbm,
    out_weight_hbm,
    result_ref,
    prior,
    observed,
    obs_weight,
    noise,
    lift_in,
    conv_in,
    out_in,
    load_sem,
    send_sem,
    recv_sem,
    state,
    main,
    edge_out,
    edge_in,
    lift_f32,
    lift_w,
    conv_w,
    out_f32,
    out_w,
    lifted,
    lifted_cols,
    activated,
    activated_cols,
):
    frames, chans, rows, cols, hidden, updates, margin = dims
    tile = frames * chans
    group = cols // rows
    span = rows + 2 * margin
    wide = cols + 2 * GUARD
    t, t_size = lax.axis_index("tm"), lax.axis_size("tm")
    l, l_size = lax.axis_index("lat"), lax.axis_size("lat")
    other = lax.rem(lax.axis_index("lon") + 1, lax.axis_size("lon"))

    loads = [
        pltpu.make_async_copy(source, target, load_sem.at[index])
        for index, (source, target) in enumerate(
            (
                (prior_hbm, prior),
                (conv_hbm, conv_in),
                (lift_hbm, lift_in),
                (out_weight_hbm, out_in),
                (observed_hbm, observed),
                (obs_weight_hbm, obs_weight),
                (noise_hbm, noise),
            )
        )
    ]
    for load in loads:
        load.start()

    main[...] = jnp.zeros_like(main)
    edge_in[...] = jnp.zeros_like(edge_in)

    around = [
        (dt, dl, do)
        for dt in (-1, 0, 1)
        for dl in (-1, 0, 1)
        for do in (0, 1)
        if (dt, dl, do) != (0, 0, 0)
    ]

    def exists(dt, dl):
        return (t + dt >= 0) & (t + dt < t_size) & (l + dl >= 0) & (l + dl < l_size)

    def target(dt, dl, do):
        own = lax.axis_index("lon")
        return {"tm": t + dt, "lat": l + dl, "lon": other if do else own}

    barrier = pltpu.get_barrier_semaphore()
    for dt, dl, do in around:

        @pl.when(exists(dt, dl))
        def _():
            pl.semaphore_signal(
                barrier, inc=1, device_id=target(dt, dl, do), device_id_type=pl.DeviceIdType.MESH
            )

    def one(flag):
        return flag.astype(jnp.int32)

    t_count = 1 + one(t > 0) + one(t < t_size - 1)
    l_count = 1 + one(l > 0) + one(l < l_size - 1)

    def message(u, dt, dl, do, chunk=0):
        slot, kind = 1 - dt, 1 - dl
        first, count = margin * chunk, margin
        if do:
            source, place = edge_out.at[u], edge_in.at[u, slot, kind]
        elif dl == 0:
            source = main.at[u, 1, pl.ds(margin + first, count)]
            place = main.at[u, slot, pl.ds(margin + first, count)]
        elif dl == 1:
            source = main.at[u, 1, pl.ds(rows, margin)]
            place = main.at[u, slot, pl.ds(0, margin)]
        else:
            source = main.at[u, 1, pl.ds(margin, margin)]
            place = main.at[u, slot, pl.ds(margin + rows, margin)]
        where = ((slot * 3 + kind) * 2 + do) * (rows // margin) + chunk
        return pltpu.make_async_remote_copy(
            src_ref=source,
            dst_ref=place,
            send_sem=send_sem.at[u, where],
            recv_sem=recv_sem.at[u, where],
            device_id=target(dt, dl, do),
            device_id_type=pl.DeviceIdType.MESH,
        )

    lane_group = lax.broadcasted_iota(jnp.int32, (tile, cols), 1) // group

    def halves(value):
        high = value.astype(BF16)
        return jnp.concatenate([high, (value - high.astype(F32)).astype(BF16)], axis=0)

    def send(u, dt, dl, do, chunk=0):
        @pl.when(exists(dt, dl))
        def _():
            message(u, dt, dl, do, chunk).start()

    def chunks_of(dl, do):
        return range(rows // margin) if dl == 0 and not do else range(1)

    def keep(u, row, value):
        state[row] = value
        main[u, 1, margin + row] = halves(value)

    def send_chunk(u, chunk):
        for dt in (-1, 1):
            send(u, dt, 0, 0, chunk)

        @pl.when(chunk == 0)
        def _():
            for dt in (-1, 0, 1):
                send(u, dt, -1, 0)

        @pl.when(chunk == rows // margin - 1)
        def _():
            for dt in (-1, 0, 1):
                send(u, dt, 1, 0)

    def send_edges(u):
        edge = jnp.zeros((tile, cols), F32)
        for row in range(rows):
            turned = pltpu.roll(state[row], (group * row + group // 2) % cols, 1)
            edge = jnp.where(lane_group == row, turned, edge)
        edge_out[u] = halves(edge)
        for dt in (-1, 0, 1):
            for dl in (-1, 0, 1):
                send(u, dt, dl, 1)

    def receive_all(u):
        for dt, dl, do in around:

            @pl.when(exists(-dt, -dl))
            def _():
                for chunk in chunks_of(dl, do):
                    message(u, dt, dl, do, chunk).wait_recv()

    def strided(frame, row):
        return pl.ds(frame * chans * rows + row, chans, stride=rows)

    loads[0].wait()
    for row in range(rows):
        keep(
            0,
            row,
            jnp.concatenate([prior[strided(frame, row), :] for frame in range(frames)], axis=0),
        )
    pl.semaphore_wait(barrier, t_count * l_count * 2 - 1)

    def send_first(chunk, carry):
        send_chunk(0, chunk)
        return carry

    lax.fori_loop(0, rows // margin, send_first, 0)
    send_edges(0)

    lift_f32[...] = jnp.zeros_like(lift_f32)
    conv_w[...] = jnp.zeros_like(conv_w)
    out_f32[...] = jnp.zeros_like(out_f32)
    lifted[...] = jnp.zeros_like(lifted)
    for load in loads[1:4]:
        load.wait()
    depth = lift_in.shape[0]
    turned = lift_in[...]
    high = turned.astype(BF16).astype(F32)
    low = turned - high
    for frame in range(frames):
        part = pl.ds(frame * LANES, hidden)
        for item in range(depth // chans):
            source = slice(item * chans, (item + 1) * chans)
            slot, place = divmod((item + frame) * chans, tile)
            lift_f32[pl.ds(slot * 2 * tile + place, chans), part] = high[source]
            lift_f32[pl.ds(slot * 2 * tile + tile + place, chans), part] = high[source]
            lift_f32[pl.ds(6 * tile + slot * tile + place, chans), part] = low[source]
    lift_w[...] = lift_f32[...].astype(BF16)
    for layer in range(2):
        for a in range(3):
            for b in range(3):
                tap = transposed(conv_in[layer, 3 * a + b]).astype(BF16)
                for q in range(2):
                    conv_w[
                        layer, pl.ds(((a + q) * 3 + b) * LANES, hidden), pl.ds(q * LANES, hidden)
                    ] = tap
    for q in range(2):
        out_f32[pl.ds(q * chans, chans), pl.ds(q * LANES, hidden)] = out_in[...].astype(F32)
    out_w[...] = out_f32[...].astype(BF16)
    for load in loads[4:]:
        load.wait()

    lane_kind = lane_group < rows // 2

    def update(u, carry):
        receive_all(u)

        def far(slot):
            low_rows = edge_in[u, slot, 2].astype(F32)
            high_rows = edge_in[u, slot, 0].astype(F32)
            kind = jnp.concatenate([lane_kind, lane_kind], axis=0)
            return jnp.where(kind, low_rows, high_rows).astype(BF16)

        sides = [main[u, slot] for slot in range(3)]
        blocks = [[sides[slot][row] for slot in range(3)] for row in range(span)]
        blocks.append([edge_in[u, slot, 1] for slot in range(3)])
        blocks.append([far(slot) for slot in range(3)])
        stacked = jnp.concatenate(
            [jnp.concatenate(block + [part[:tile] for part in block], axis=0) for block in blocks],
            axis=1,
        )
        result = lax.dot_general(
            stacked, lift_w[...], (((0,), (0,)), ((), ())), preferred_element_type=F32
        )
        result = result.astype(BF16).astype(F32)
        own_edge = result[span * cols : (span + 1) * cols]
        far_edge = result[(span + 1) * cols :]
        for row in range(span):
            if row < margin:
                start, edge = group * (rows - margin + row), far_edge
            elif row < margin + rows:
                start, edge = group * (row - margin), own_edge
            else:
                start, edge = group * (row - margin - rows), far_edge
            middle = start + group // 2
            lifted[row, pl.ds(GUARD, cols)] = result[row * cols : (row + 1) * cols]
            lifted[row, pl.ds(0, GUARD)] = edge[middle - GUARD : middle]
            lifted[row, pl.ds(GUARD + cols, GUARD)] = edge[middle : middle + GUARD]
        for row in range(span):
            for b in range(3):
                for frame in range(frames):
                    part = pl.ds(frame * LANES, LANES)
                    lifted_cols[b, row % 2, row // 2, frame] = lifted[
                        row, pl.ds(GUARD - 2 + b, wide), part
                    ].astype(BF16)

        top = jnp.where(l == 0, 0.0, 1.0).astype(F32)
        bottom = jnp.where(l == l_size - 1, 0.0, 1.0).astype(F32)
        pairs = rows // 2 + 1

        def first_conv(pair, carry):
            above = jnp.where(pair == 0, top, 1.0)
            below = jnp.where(pair == pairs - 1, bottom, 1.0)
            window = jnp.concatenate(
                [
                    lifted_cols[b, r % 2, pair + r // 2].reshape(frames * wide, LANES)
                    for r in range(4)
                    for b in range(3)
                ],
                axis=1,
            )
            result = silu(jnp.dot(window, conv_w[0], preferred_element_type=F32))
            for frame in range(frames):
                for q in range(2):
                    value = result[frame * wide : (frame + 1) * wide, q * LANES : (q + 1) * LANES]
                    value = value * (below if q else above)
                    activated[frame, 2 * pair + q] = value
                    for b in range(3):
                        activated_cols[b, q, pair, frame] = activated[
                            frame, 2 * pair + q, pl.ds(b, cols)
                        ].astype(BF16)
            return carry

        lax.fori_loop(0, pairs, first_conv, 0)

        step = jnp.full((chans, cols), steps_ref[u], F32)
        spread = jnp.sqrt(2.0 * step)

        def second_conv(pair, carry):
            window = jnp.concatenate(
                [
                    activated_cols[b, r % 2, pair + r // 2].reshape(frames * cols, LANES)
                    for r in range(4)
                    for b in range(3)
                ],
                axis=1,
            )
            second = silu(jnp.dot(window, conv_w[1], preferred_element_type=F32))
            base = jnp.concatenate(
                [
                    jnp.concatenate(
                        [
                            lifted[
                                margin + 2 * pair + q, pl.ds(GUARD, cols), pl.ds(frame * LANES, LANES)
                            ]
                            for q in range(2)
                        ],
                        axis=1,
                    )
                    for frame in range(frames)
                ],
                axis=0,
            )
            merged = (base + second).astype(BF16)
            score = lax.dot_general(
                out_w[...], merged, (((1,), (1,)), ((), ())), preferred_element_type=F32
            )
            for q in range(2):
                row = 2 * pair + q
                fresh = []
                for frame in range(frames):
                    where = strided(frame, row)
                    current = state[row, pl.ds(frame * chans, chans)]
                    drift = score[q * chans : (q + 1) * chans, frame * cols : (frame + 1) * cols]
                    pull = obs_weight[where, :] * (observed[where, :] - current)
                    value = current + step * (drift + pull) + spread * noise[u, where, :]
                    fresh.append(value)
                    result_ref[where, :] = value
                keep(u + 1, row, jnp.concatenate(fresh, axis=0))

            @pl.when(u < updates - 1)
            def _():
                send_chunk(u + 1, pair)

            return carry

        lax.fori_loop(0, rows // 2, second_conv, 0)

        @pl.when(u < updates - 1)
        def _():
            send_edges(u + 1)

        return carry

    lax.fori_loop(0, updates, update, 0)

    for u in range(updates):
        for dt, dl, do in around:

            @pl.when(exists(dt, dl))
            def _():
                for chunk in chunks_of(dl, do):
                    message(u, dt, dl, do, chunk).wait_send()


def per_device(
    prior_state, observed, obs_weight, noise_field, step_sizes, lift_weight, conv_weights, out_weight
):
    frames, chans, rows, cols = prior_state.shape
    hidden, depth = lift_weight.shape
    updates = noise_field.shape[0]
    margin = 2
    tile = frames * chans
    span = rows + 2 * margin
    wide = cols + 2 * GUARD
    flat = (tile * rows, cols)
    dims = (frames, chans, rows, cols, hidden, updates, margin)
    vmem = pltpu.VMEM
    result = pl.pallas_call(
        functools.partial(kernel, dims),
        out_shape=jax.ShapeDtypeStruct(flat, F32),
        in_specs=[pl.BlockSpec(memory_space=pltpu.SMEM)] + [pl.BlockSpec(memory_space=pl.ANY)] * 7,
        out_specs=pl.BlockSpec(memory_space=pltpu.VMEM),
        scratch_shapes=[
            vmem(flat, F32),
            vmem(flat, F32),
            vmem(flat, F32),
            vmem((updates, *flat), F32),
            vmem((depth, hidden), F32),
            vmem(conv_weights.shape, BF16),
            vmem(out_weight.shape, BF16),
            pltpu.SemaphoreType.DMA((7,)),
            pltpu.SemaphoreType.DMA((updates, 18 * (rows // margin))),
            pltpu.SemaphoreType.DMA((updates, 18 * (rows // margin))),
            vmem((rows, tile, cols), F32),
            vmem((updates + 1, 3, span, 2 * tile, cols), BF16),
            vmem((updates, 2 * tile, cols), BF16),
            vmem((updates, 3, 3, 2 * tile, cols), BF16),
            vmem((9 * tile, frames * LANES), F32),
            vmem((9 * tile, frames * LANES), BF16),
            vmem((2, 12 * LANES, 2 * LANES), BF16),
            vmem((2 * chans, 2 * LANES), F32),
            vmem((2 * chans, 2 * LANES), BF16),
            vmem((span, wide + GUARD, frames * LANES), F32),
            vmem((3, 2, span // 2, frames, wide, LANES), BF16),
            vmem((frames, rows + 2, wide, LANES), F32),
            vmem((3, 2, rows // 2 + 1, frames, cols, LANES), BF16),
        ],
        compiler_params=pltpu.CompilerParams(
            collective_id=0, has_side_effects=True, vmem_limit_bytes=60 * 1024 * 1024
        ),
        cost_estimate=pl.CostEstimate(
            flops=4 * updates * tile * rows * cols * hidden * 9 * hidden // chans,
            bytes_accessed=1 << 20,
            transcendentals=0,
        ),
    )(
        step_sizes,
        prior_state.reshape(flat),
        observed.reshape(flat),
        obs_weight.reshape(flat),
        noise_field.reshape(updates, *flat),
        lift_weight.T,
        conv_weights,
        out_weight,
    )
    return result.reshape(prior_state.shape)


def solution(mesh):
    placed = (
        P(("groups", "tm"), None, "lat", "lon"),
        P(("groups", "tm"), None, "lat", "lon"),
        P(("groups", "tm"), None, "lat", "lon"),
        P(None, ("groups", "tm"), None, "lat", "lon"),
        P(),
        P(),
        P(),
        P(),
    )
    return jax.shard_map(
        per_device,
        mesh=mesh,
        in_specs=placed,
        out_specs=P(("groups", "tm"), None, "lat", "lon"),
        check_vma=False,
    )
```

```python
import functools

import jax
import jax.numpy as jnp
from jax import lax
from jax.experimental import pallas as pl
from jax.experimental.pallas import tpu as pltpu
from jax.sharding import PartitionSpec as P

F32 = jnp.float32
BF16 = jnp.bfloat16
LANES = 128


def silu(value):
    half = 0.5 * value
    return half + half * jnp.tanh(half)


def kernel(
    dims,
    steps_ref,
    prior_hbm,
    observed_hbm,
    obs_weight_hbm,
    noise_hbm,
    lift_hbm,
    conv_hbm,
    out_weight_hbm,
    result_ref,
    prior,
    observed,
    obs_weight,
    noise,
    lift_in,
    conv_in,
    out_in,
    load_sem,
    send_sem,
    recv_sem,
    state,
    main,
    edge_out,
    edge_in,
    lift_f32,
    lift_w,
    conv_w,
    out_w,
    lifted_cols,
    activated_cols,
):
    frames, chans, rows, cols, hidden, updates, margin = dims
    tile = frames * chans
    group = cols // rows
    span = rows + 2 * margin
    t, t_size = lax.axis_index("tm"), lax.axis_size("tm")
    l, l_size = lax.axis_index("lat"), lax.axis_size("lat")
    other = lax.rem(lax.axis_index("lon") + 1, lax.axis_size("lon"))

    loads = [
        pltpu.make_async_copy(source, target, load_sem.at[index])
        for index, (source, target) in enumerate(
            (
                (prior_hbm, prior),
                (conv_hbm, conv_in),
                (lift_hbm, lift_in),
                (out_weight_hbm, out_in),
                (observed_hbm, observed),
                (obs_weight_hbm, obs_weight),
                (noise_hbm, noise),
            )
        )
    ]
    for load in loads:
        load.start()

    main[...] = jnp.zeros_like(main)
    edge_in[...] = jnp.zeros_like(edge_in)

    around = [
        (dt, dl, do)
        for dt in (-1, 0, 1)
        for dl in (-1, 0, 1)
        for do in (0, 1)
        if (dt, dl, do) != (0, 0, 0)
    ]

    def exists(dt, dl):
        return (t + dt >= 0) & (t + dt < t_size) & (l + dl >= 0) & (l + dl < l_size)

    def target(dt, dl, do):
        own = lax.axis_index("lon")
        return {"tm": t + dt, "lat": l + dl, "lon": other if do else own}

    barrier = pltpu.get_barrier_semaphore()
    for dt, dl, do in around:

        @pl.when(exists(dt, dl))
        def _():
            pl.semaphore_signal(
                barrier, inc=1, device_id=target(dt, dl, do), device_id_type=pl.DeviceIdType.MESH
            )

    def one(flag):
        return flag.astype(jnp.int32)

    t_count = 1 + one(t > 0) + one(t < t_size - 1)
    l_count = 1 + one(l > 0) + one(l < l_size - 1)

    def message(u, dt, dl, do, chunk=0):
        slot, kind = 1 - dt, 1 - dl
        first, count = margin * chunk, margin
        if do:
            source, place = edge_out.at[u], edge_in.at[u, slot, kind, do - 1]
        elif dl == 0:
            source = main.at[u, 1, pl.ds(margin + first, count)]
            place = main.at[u, slot, pl.ds(margin + first, count)]
        elif dl == 1:
            source = main.at[u, 1, pl.ds(rows, margin)]
            place = main.at[u, slot, pl.ds(0, margin)]
        else:
            source = main.at[u, 1, pl.ds(margin, margin)]
            place = main.at[u, slot, pl.ds(margin + rows, margin)]
        where = ((slot * 3 + kind) * 3 + do) * (rows // margin) + chunk
        return pltpu.make_async_remote_copy(
            src_ref=source,
            dst_ref=place,
            send_sem=send_sem.at[u, where],
            recv_sem=recv_sem.at[u, where],
            device_id=target(dt, dl, do == 1),
            device_id_type=pl.DeviceIdType.MESH,
        )

    lane = lax.broadcasted_iota(jnp.int32, (tile, cols), 1)
    lane_group = lane // group
    lane_half = lane % group < group // 2

    def halves(value):
        high = value.astype(BF16)
        return jnp.concatenate([high, (value - high.astype(F32)).astype(BF16)], axis=0)

    def send(u, dt, dl, do, chunk=0):
        @pl.when(exists(dt, dl))
        def _():
            message(u, dt, dl, do, chunk).start()

    def chunks_of(dl, do):
        return range(rows // margin) if dl == 0 and not do else range(1)

    def keep(u, row, value):
        state[row] = value
        main[u, 1, margin + row] = halves(value)

    def send_chunk(u, chunk):
        for dt in (-1, 1):
            send(u, dt, 0, 0, chunk)

        if chunk == 0:
            for dt in (-1, 0, 1):
                send(u, dt, -1, 0)
        if chunk == rows // margin - 1:
            for dt in (-1, 0, 1):
                send(u, dt, 1, 0)

    def send_edges(u):
        edge = jnp.zeros((tile, cols), F32)
        for row in range(rows):
            value = state[row]
            first = pltpu.roll(value, (group * row + group // 4) % cols, 1)
            last = pltpu.roll(value, (group * row + 3 * group // 4) % cols, 1)
            edge = jnp.where(lane_group == row, jnp.where(lane_half, first, last), edge)
        edge_out[u] = halves(edge)
        for dt in (-1, 0, 1):
            for dl in (-1, 0, 1):
                send(u, dt, dl, 1)
                if dt or dl:
                    send(u, dt, dl, 2)

    sent = around + [(dt, dl, 2) for dt, dl, do in around if not do]

    def receive_all(u):
        for dt, dl, do in sent:

            @pl.when(exists(-dt, -dl))
            def _():
                for chunk in chunks_of(dl, do):
                    message(u, dt, dl, do, chunk).wait_recv()

    def strided(frame, row):
        return pl.ds(frame * chans * rows + row, chans, stride=rows)

    loads[0].wait()
    for row in range(rows):
        keep(
            0,
            row,
            jnp.concatenate([prior[strided(frame, row), :] for frame in range(frames)], axis=0),
        )
    pl.semaphore_wait(barrier, t_count * l_count * 2 - 1)

    for chunk in range(rows // margin):
        send_chunk(0, chunk)
    send_edges(0)

    lift_f32[...] = jnp.zeros_like(lift_f32)
    for load in loads[1:4]:
        load.wait()
    depth = lift_in.shape[0]
    turned = lift_in[...]
    high = turned.astype(BF16).astype(F32)
    low = turned - high
    for frame in range(frames):
        part = pl.ds(frame * LANES, hidden)
        for item in range(depth // chans):
            source = slice(item * chans, (item + 1) * chans)
            slot, place = divmod((item + frame) * chans, tile)
            lift_f32[pl.ds(slot * 2 * tile + place, chans), part] = high[source]
            lift_f32[pl.ds(slot * 2 * tile + tile + place, chans), part] = high[source]
            lift_f32[pl.ds(6 * tile + slot * tile + place, chans), part] = low[source]
    turned = jnp.transpose(lift_f32[...])
    for frame in range(frames):
        lift_w[pl.ds(frame * hidden, hidden)] = turned[
            frame * LANES : frame * LANES + hidden
        ].astype(BF16)
    for layer in range(2):
        taps = [conv_in[layer, tap] for tap in range(9)]
        empty = [jnp.zeros((hidden, hidden), BF16)] * 3
        conv_w[layer, pl.ds(0, hidden)] = jnp.concatenate(taps + empty, axis=1)
        conv_w[layer, pl.ds(hidden, hidden)] = jnp.concatenate(empty + taps, axis=1)
    project = out_in[...].astype(F32)
    blank = jnp.zeros_like(project)
    out_w[...] = jnp.concatenate(
        [jnp.concatenate([project, blank], axis=1), jnp.concatenate([blank, project], axis=1)],
        axis=0,
    ).astype(BF16)
    for load in loads[4:]:
        load.wait()

    lane_tall = lax.broadcasted_iota(jnp.int32, (2 * tile, cols), 1)
    own_lanes = (lane_tall % group >= group // 4) & (lane_tall % group < 3 * group // 4)
    low_lanes = lane_tall < cols // 2
    edge_lane = lax.broadcasted_iota(jnp.int32, (hidden, 2 * cols), 1)

    def shifted(value, edge, row, b):
        first = (group * row + group // 4 - 1) % (2 * cols)
        last = (group * row + 3 * group // 4) % (2 * cols)
        if b == 0:
            return jnp.concatenate([edge[:, first : first + 1], value[:, : cols - 1]], axis=1)
        if b == 2:
            return jnp.concatenate([value[:, 1:], edge[:, last : last + 1]], axis=1)
        return value

    def update(u, carry):
        receive_all(u)

        def rim(slot, kind):
            same = edge_out[u] if (slot, kind) == (1, 1) else edge_in[u, slot, kind, 1]
            return jnp.where(own_lanes, same.astype(F32), edge_in[u, slot, kind, 0].astype(F32))

        blocks = [[main[u, slot, row] for slot in range(3)] for row in range(span)]
        blocks.append([rim(slot, 1).astype(BF16) for slot in range(3)])
        blocks.append(
            [jnp.where(low_lanes, rim(slot, 2), rim(slot, 0)).astype(BF16) for slot in range(3)]
        )
        stacked = jnp.concatenate(
            [jnp.concatenate(block + [part[:tile] for part in block], axis=0) for block in blocks],
            axis=1,
        )
        result = jnp.dot(lift_w[...], stacked, preferred_element_type=F32).astype(BF16)
        edges = []
        for frame in range(frames):
            whole = result[frame * hidden : (frame + 1) * hidden]
            part = pl.ds(frame * cols, cols)
            edge = whole[:, span * cols :]
            edges.append(edge)
            for row in range(span):
                value = whole[:, row * cols : (row + 1) * cols]
                for b in range(3):
                    lifted_cols[b, row, :, part] = shifted(value, edge, row - margin, b)

        top = jnp.where(l == 0, 0.0, 1.0).astype(F32)
        bottom = jnp.where(l == l_size - 1, 0.0, 1.0).astype(F32)
        pairs = rows // 2 + 1
        for frame in range(frames):
            turns = []
            for a in range(-1, 2):
                for b in range(-1, 2):
                    turn = (group * a + b) % (2 * cols)
                    edge = edges[frame]
                    if turn:
                        edge = jnp.concatenate([edge[:, turn:], edge[:, :turn]], axis=1)
                    turns.append(edge)
            value = silu(
                jnp.dot(
                    conv_w[0, pl.ds(0, hidden), pl.ds(0, 9 * hidden)],
                    jnp.concatenate(turns, axis=0),
                    preferred_element_type=F32,
                )
            )
            value = jnp.where(edge_lane >= 2 * cols - group, value * top, value)
            after = (edge_lane >= cols) & (edge_lane < cols + group)
            edges[frame] = jnp.where(after, value * bottom, value).astype(BF16)

        for pair in range(pairs):
            window = jnp.concatenate(
                [lifted_cols[b, 2 * pair + r] for r in range(4) for b in range(3)], axis=0
            )
            result = silu(jnp.dot(conv_w[0], window, preferred_element_type=F32))
            for q in range(2):
                value = result[q * hidden : (q + 1) * hidden]
                if pair == 0 and q == 0:
                    value = value * top
                if pair == pairs - 1 and q == 1:
                    value = value * bottom
                value = value.astype(BF16)
                row = 2 * pair + q
                for frame in range(frames):
                    own = value[:, frame * cols : (frame + 1) * cols]
                    for b in range(3):
                        activated_cols[b, row, :, pl.ds(frame * cols, cols)] = shifted(
                            own, edges[frame], row - 1, b
                        )

        step = jnp.full((chans, cols), steps_ref[u], F32)
        spread = jnp.sqrt(2.0 * step)

        for pair in range(rows // 2):
            window = jnp.concatenate(
                [activated_cols[b, 2 * pair + r] for r in range(4) for b in range(3)], axis=0
            )
            second = silu(jnp.dot(conv_w[1], window, preferred_element_type=F32))
            base = jnp.concatenate(
                [lifted_cols[1, margin + 2 * pair + q] for q in range(2)], axis=0
            )
            merged = (base.astype(F32) + second).astype(BF16)
            score = jnp.dot(out_w[...], merged, preferred_element_type=F32)
            for q in range(2):
                row = 2 * pair + q
                fresh = []
                for frame in range(frames):
                    where = strided(frame, row)
                    current = state[row, pl.ds(frame * chans, chans)]
                    drift = score[q * chans : (q + 1) * chans, frame * cols : (frame + 1) * cols]
                    pull = obs_weight[where, :] * (observed[where, :] - current)
                    value = current + step * (drift + pull) + spread * noise[u, where, :]
                    fresh.append(value)
                    result_ref[where, :] = value
                keep(u + 1, row, jnp.concatenate(fresh, axis=0))

            @pl.when(u < updates - 1)
            def _():
                send_chunk(u + 1, pair)

        @pl.when(u < updates - 1)
        def _():
            send_edges(u + 1)

        return carry

    lax.fori_loop(0, updates, update, 0)

    for u in range(updates):
        for dt, dl, do in sent:

            @pl.when(exists(dt, dl))
            def _():
                for chunk in chunks_of(dl, do):
                    message(u, dt, dl, do, chunk).wait_send()


def per_device(
    prior_state, observed, obs_weight, noise_field, step_sizes, lift_weight, conv_weights, out_weight
):
    frames, chans, rows, cols = prior_state.shape
    hidden, depth = lift_weight.shape
    updates = noise_field.shape[0]
    margin = 2
    tile = frames * chans
    span = rows + 2 * margin
    flat = (tile * rows, cols)
    dims = (frames, chans, rows, cols, hidden, updates, margin)
    vmem = pltpu.VMEM
    result = pl.pallas_call(
        functools.partial(kernel, dims),
        out_shape=jax.ShapeDtypeStruct(flat, F32),
        in_specs=[pl.BlockSpec(memory_space=pltpu.SMEM)] + [pl.BlockSpec(memory_space=pl.ANY)] * 7,
        out_specs=pl.BlockSpec(memory_space=pltpu.VMEM),
        scratch_shapes=[
            vmem(flat, F32),
            vmem(flat, F32),
            vmem(flat, F32),
            vmem((updates, *flat), F32),
            vmem((depth, hidden), F32),
            vmem(conv_weights.shape, BF16),
            vmem(out_weight.shape, BF16),
            pltpu.SemaphoreType.DMA((7,)),
            pltpu.SemaphoreType.DMA((updates, 27 * (rows // margin))),
            pltpu.SemaphoreType.DMA((updates, 27 * (rows // margin))),
            vmem((rows, tile, cols), F32),
            vmem((updates + 1, 3, span, 2 * tile, cols), BF16),
            vmem((updates, 2 * tile, cols), BF16),
            vmem((updates, 3, 3, 2, 2 * tile, cols), BF16),
            vmem((9 * tile, frames * LANES), F32),
            vmem((frames * hidden, 9 * tile), BF16),
            vmem((2, 2 * hidden, 12 * hidden), BF16),
            vmem((2 * chans, 2 * hidden), BF16),
            vmem((3, span, hidden, frames * cols), BF16),
            vmem((3, rows + 2, hidden, frames * cols), BF16),
        ],
        compiler_params=pltpu.CompilerParams(
            collective_id=0, has_side_effects=True, vmem_limit_bytes=60 * 1024 * 1024
        ),
        cost_estimate=pl.CostEstimate(
            flops=4 * updates * tile * rows * cols * hidden * 9 * hidden // chans,
            bytes_accessed=1 << 20,
            transcendentals=0,
        ),
    )(
        step_sizes,
        prior_state.reshape(flat),
        observed.reshape(flat),
        obs_weight.reshape(flat),
        noise_field.reshape(updates, *flat),
        lift_weight.T,
        conv_weights,
        out_weight,
    )
    return result.reshape(prior_state.shape)


def solution(mesh):
    placed = (
        P(("groups", "tm"), None, "lat", "lon"),
        P(("groups", "tm"), None, "lat", "lon"),
        P(("groups", "tm"), None, "lat", "lon"),
        P(None, ("groups", "tm"), None, "lat", "lon"),
        P(),
        P(),
        P(),
        P(),
    )
    return jax.shard_map(
        per_device,
        mesh=mesh,
        in_specs=placed,
        out_specs=P(("groups", "tm"), None, "lat", "lon"),
        check_vma=False,
    )
```

```python
import functools

import jax
import jax.numpy as jnp
from jax import lax
from jax.experimental import pallas as pl
from jax.experimental.pallas import tpu as pltpu
from jax.sharding import PartitionSpec as P

F32 = jnp.float32
BF16 = jnp.bfloat16
LANES = 128


def silu(value):
    half = 0.5 * value
    return half + half * jnp.tanh(half)


def kernel(
    dims,
    steps_ref,
    prior_hbm,
    observed_hbm,
    obs_weight_hbm,
    noise_hbm,
    lift_hbm,
    conv_hbm,
    out_weight_hbm,
    result_ref,
    prior,
    observed,
    obs_weight,
    noise,
    lift_in,
    conv_in,
    out_in,
    load_sem,
    send_sem,
    recv_sem,
    state,
    main,
    edge_in,
    lift_f32,
    lift_w,
    conv_w,
    out_w,
    lifted_cols,
    activated_cols,
):
    frames, chans, rows, cols, hidden, updates, margin = dims
    tile = frames * chans
    group = cols // rows
    span = rows + 2 * margin
    t, t_size = lax.axis_index("tm"), lax.axis_size("tm")
    l, l_size = lax.axis_index("lat"), lax.axis_size("lat")
    other = lax.rem(lax.axis_index("lon") + 1, lax.axis_size("lon"))

    loads = [
        pltpu.make_async_copy(source, target, load_sem.at[index])
        for index, (source, target) in enumerate(
            (
                (prior_hbm, prior),
                (conv_hbm, conv_in),
                (lift_hbm, lift_in),
                (out_weight_hbm, out_in),
                (observed_hbm, observed),
                (obs_weight_hbm, obs_weight),
                (noise_hbm, noise),
            )
        )
    ]
    for load in loads:
        load.start()

    head = margin + 1
    own_start = head + 1
    own_edge = own_start + rows
    tail = own_edge + 1

    def cleared(ref):
        ref[...] = jnp.zeros(ref.shape, ref.dtype)

    for u in range(updates):
        for slot, absent in ((0, t == 0), (2, t == t_size - 1)):

            @pl.when(absent)
            def _():
                cleared(main.at[u, slot])
                cleared(edge_in.at[u, slot])

        for kind, first, absent in ((0, 0, l == 0), (2, tail, l == l_size - 1)):

            @pl.when(absent)
            def _():
                for slot in range(3):
                    cleared(main.at[u, slot, pl.ds(first, head)])
                    cleared(edge_in.at[u, slot, kind])


    around = [
        (dt, dl, do)
        for dt in (-1, 0, 1)
        for dl in (-1, 0, 1)
        for do in (0, 1)
        if (dt, dl, do) != (0, 0, 0)
    ]

    def exists(dt, dl):
        return (t + dt >= 0) & (t + dt < t_size) & (l + dl >= 0) & (l + dl < l_size)

    def target(dt, dl, do):
        own = lax.axis_index("lon")
        return {"tm": t + dt, "lat": l + dl, "lon": other if do else own}

    barrier = pltpu.get_barrier_semaphore()
    for dt, dl, do in around:

        @pl.when(exists(dt, dl))
        def _():
            pl.semaphore_signal(
                barrier, inc=1, device_id=target(dt, dl, do), device_id_type=pl.DeviceIdType.MESH
            )

    def one(flag):
        return flag.astype(jnp.int32)

    t_count = 1 + one(t > 0) + one(t < t_size - 1)
    l_count = 1 + one(l > 0) + one(l < l_size - 1)

    def message(u, dt, dl, do, chunk=0):
        slot, kind = 1 - dt, 1 - dl
        if do:
            source, place = main.at[u, 1, own_edge], edge_in.at[u, slot, kind]
        else:
            if dl == 1 or (dl == 0 and chunk == 1):
                first, count = own_edge - margin, head
            elif dl == 0:
                first, count = own_start, rows - margin
            else:
                first, count = head, head
            landing = {1: 0, 0: first, -1: tail}[dl]
            source = main.at[u, 1, pl.ds(first, count)]
            place = main.at[u, slot, pl.ds(landing, count)]
        where = ((slot * 3 + kind) * 2 + do) * 2 + chunk
        return pltpu.make_async_remote_copy(
            src_ref=source,
            dst_ref=place,
            send_sem=send_sem.at[u, where],
            recv_sem=recv_sem.at[u, where],
            device_id=target(dt, dl, do),
            device_id_type=pl.DeviceIdType.MESH,
        )

    lane = lax.broadcasted_iota(jnp.int32, (tile, cols), 1)
    lane_group = lane // group
    lane_half = lane % group < group // 2

    def halves(value):
        high = value.astype(BF16)
        return jnp.concatenate([high, (value - high.astype(F32)).astype(BF16)], axis=0)

    def send(u, dt, dl, do, chunk=0):
        @pl.when(exists(dt, dl))
        def _():
            message(u, dt, dl, do, chunk).start()

    def chunks_of(dl, do):
        return range(2) if dl == 0 and not do else range(1)

    def keep(u, row, value):
        state[row] = value
        main[u, 1, own_start + row] = halves(value)

    def send_early(u):
        for dt in (-1, 1):
            send(u, dt, 0, 0, 0)

    def send_edges(u):
        edge = jnp.zeros((tile, cols), F32)
        for row in range(rows):
            value = state[row]
            first = pltpu.roll(value, (group * row + group // 4) % cols, 1)
            last = pltpu.roll(value, (group * row + 3 * group // 4) % cols, 1)
            edge = jnp.where(lane_group == row, jnp.where(lane_half, first, last), edge)
        main[u, 1, head] = halves(edge)
        main[u, 1, own_edge] = halves(edge)
        for dt in (-1, 1):
            send(u, dt, 0, 0, 1)
        for dt in (-1, 1, 0):
            for dl in (-1, 1):
                send(u, dt, dl, 0)
            for dl in (-1, 1, 0):
                send(u, dt, dl, 1)

    def receive_all(u):
        for dt, dl, do in around:

            @pl.when(exists(-dt, -dl))
            def _():
                for chunk in chunks_of(dl, do):
                    message(u, dt, dl, do, chunk).wait_recv()

    def strided(frame, row):
        return pl.ds(frame * chans * rows + row, chans, stride=rows)

    loads[0].wait()
    for row in range(rows):
        keep(
            0,
            row,
            jnp.concatenate([prior[strided(frame, row), :] for frame in range(frames)], axis=0),
        )
    pl.semaphore_wait(barrier, t_count * l_count * 2 - 1)

    send_early(0)
    send_edges(0)

    lift_f32[...] = jnp.zeros_like(lift_f32)
    for load in loads[1:4]:
        load.wait()
    depth = lift_in.shape[0]
    turned = lift_in[...]
    high = turned.astype(BF16).astype(F32)
    low = turned - high
    for frame in range(frames):
        part = pl.ds(frame * LANES, hidden)
        for item in range(depth // chans):
            source = slice(item * chans, (item + 1) * chans)
            slot, place = divmod((item + frame) * chans, tile)
            lift_f32[pl.ds(slot * 2 * tile + place, chans), part] = high[source]
            lift_f32[pl.ds(slot * 2 * tile + tile + place, chans), part] = high[source]
            lift_f32[pl.ds(6 * tile + slot * tile + place, chans), part] = low[source]
    turned = jnp.transpose(lift_f32[...])
    for frame in range(frames):
        lift_w[pl.ds(frame * hidden, hidden)] = turned[
            frame * LANES : frame * LANES + hidden
        ].astype(BF16)
    for layer in range(2):
        taps = [conv_in[layer, tap] for tap in range(9)]
        empty = [jnp.zeros((hidden, hidden), BF16)] * 3
        conv_w[layer, pl.ds(0, hidden)] = jnp.concatenate(taps + empty, axis=1)
        conv_w[layer, pl.ds(hidden, hidden)] = jnp.concatenate(empty + taps, axis=1)
    project = out_in[...].astype(F32)
    blank = jnp.zeros_like(project)
    out_w[...] = jnp.concatenate(
        [jnp.concatenate([project, blank], axis=1), jnp.concatenate([blank, project], axis=1)],
        axis=0,
    ).astype(BF16)
    for load in loads[4:]:
        load.wait()

    lane_tall = lax.broadcasted_iota(jnp.int32, (2 * tile, cols), 1)
    own_lanes = (lane_tall % group >= group // 4) & (lane_tall % group < 3 * group // 4)
    low_lanes = lane_tall < cols // 2
    edge_lane = lax.broadcasted_iota(jnp.int32, (hidden, 2 * cols), 1)

    def shifted(value, edge, row, b):
        first = (group * row + group // 4 - 1) % (2 * cols)
        last = (group * row + 3 * group // 4) % (2 * cols)
        if b == 0:
            return jnp.concatenate([edge[:, first : first + 1], value[:, : cols - 1]], axis=1)
        if b == 2:
            return jnp.concatenate([value[:, 1:], edge[:, last : last + 1]], axis=1)
        return value

    def update(u, carry):
        receive_all(u)

        def rim(slot, kind):
            same = main[u, slot, (margin, own_edge, tail)[kind]]
            return jnp.where(own_lanes, same.astype(F32), edge_in[u, slot, kind].astype(F32))

        tiles = [
            row + (2 if row >= margin else 0) + (2 if row >= margin + rows else 0)
            for row in range(span)
        ]
        blocks = [[main[u, slot, place] for slot in range(3)] for place in tiles]
        blocks.append([rim(slot, 1).astype(BF16) for slot in range(3)])
        blocks.append(
            [jnp.where(low_lanes, rim(slot, 2), rim(slot, 0)).astype(BF16) for slot in range(3)]
        )
        stacked = jnp.concatenate(
            [jnp.concatenate(block + [part[:tile] for part in block], axis=0) for block in blocks],
            axis=1,
        )
        result = jnp.dot(lift_w[...], stacked, preferred_element_type=F32).astype(BF16)
        edges = []
        for frame in range(frames):
            whole = result[frame * hidden : (frame + 1) * hidden]
            part = pl.ds(frame * cols, cols)
            edge = whole[:, span * cols :]
            edges.append(edge)
            for row in range(span):
                value = whole[:, row * cols : (row + 1) * cols]
                for b in range(3):
                    lifted_cols[b, row, :, part] = shifted(value, edge, row - margin, b)

        top = jnp.where(l == 0, 0.0, 1.0).astype(F32)
        bottom = jnp.where(l == l_size - 1, 0.0, 1.0).astype(F32)
        pairs = rows // 2 + 1
        for frame in range(frames):
            turns = []
            for a in range(-1, 2):
                for b in range(-1, 2):
                    turn = (group * a + b) % (2 * cols)
                    edge = edges[frame]
                    if turn:
                        edge = jnp.concatenate([edge[:, turn:], edge[:, :turn]], axis=1)
                    turns.append(edge)
            value = silu(
                jnp.dot(
                    conv_w[0, pl.ds(0, hidden), pl.ds(0, 9 * hidden)],
                    jnp.concatenate(turns, axis=0),
                    preferred_element_type=F32,
                )
            )
            value = jnp.where(edge_lane >= 2 * cols - group, value * top, value)
            after = (edge_lane >= cols) & (edge_lane < cols + group)
            edges[frame] = jnp.where(after, value * bottom, value).astype(BF16)

        for pair in range(pairs):
            window = jnp.concatenate(
                [lifted_cols[b, 2 * pair + r] for r in range(4) for b in range(3)], axis=0
            )
            result = silu(jnp.dot(conv_w[0], window, preferred_element_type=F32))
            for q in range(2):
                value = result[q * hidden : (q + 1) * hidden]
                if pair == 0 and q == 0:
                    value = value * top
                if pair == pairs - 1 and q == 1:
                    value = value * bottom
                value = value.astype(BF16)
                row = 2 * pair + q
                for frame in range(frames):
                    own = value[:, frame * cols : (frame + 1) * cols]
                    for b in range(3):
                        activated_cols[b, row, :, pl.ds(frame * cols, cols)] = shifted(
                            own, edges[frame], row - 1, b
                        )

        step = jnp.full((chans, cols), steps_ref[u], F32)
        spread = jnp.sqrt(2.0 * step)

        for pair in range(rows // 2):
            window = jnp.concatenate(
                [activated_cols[b, 2 * pair + r] for r in range(4) for b in range(3)], axis=0
            )
            second = silu(jnp.dot(conv_w[1], window, preferred_element_type=F32))
            base = jnp.concatenate(
                [lifted_cols[1, margin + 2 * pair + q] for q in range(2)], axis=0
            )
            merged = (base.astype(F32) + second).astype(BF16)
            score = jnp.dot(out_w[...], merged, preferred_element_type=F32)
            fresh_rows = []
            for q in range(2):
                row = 2 * pair + q
                fresh = []
                for frame in range(frames):
                    where = strided(frame, row)
                    current = state[row, pl.ds(frame * chans, chans)]
                    drift = score[q * chans : (q + 1) * chans, frame * cols : (frame + 1) * cols]
                    pull = obs_weight[where, :] * (observed[where, :] - current)
                    value = current + step * (drift + pull) + spread * noise[u, where, :]
                    fresh.append(value)
                    result_ref[where, :] = value
                fresh_rows.append(jnp.concatenate(fresh, axis=0))

            @pl.when(u < updates - 1)
            def _():
                for q in range(2):
                    keep(u + 1, 2 * pair + q, fresh_rows[q])
                if pair == rows // 2 - 2:
                    send_early(u + 1)

        @pl.when(u < updates - 1)
        def _():
            send_edges(u + 1)

        return carry

    lax.fori_loop(0, updates, update, 0)

    for u in range(updates):
        for dt, dl, do in around:

            @pl.when(exists(dt, dl))
            def _():
                for chunk in chunks_of(dl, do):
                    message(u, dt, dl, do, chunk).wait_send()


def per_device(
    prior_state, observed, obs_weight, noise_field, step_sizes, lift_weight, conv_weights, out_weight
):
    frames, chans, rows, cols = prior_state.shape
    hidden, depth = lift_weight.shape
    updates = noise_field.shape[0]
    margin = 2
    tile = frames * chans
    span = rows + 2 * margin
    flat = (tile * rows, cols)
    dims = (frames, chans, rows, cols, hidden, updates, margin)
    vmem = pltpu.VMEM
    result = pl.pallas_call(
        functools.partial(kernel, dims),
        out_shape=jax.ShapeDtypeStruct(flat, F32),
        in_specs=[pl.BlockSpec(memory_space=pltpu.SMEM)] + [pl.BlockSpec(memory_space=pl.ANY)] * 7,
        out_specs=pl.BlockSpec(memory_space=pltpu.VMEM),
        scratch_shapes=[
            vmem(flat, F32),
            vmem(flat, F32),
            vmem(flat, F32),
            vmem((updates, *flat), F32),
            vmem((depth, hidden), F32),
            vmem(conv_weights.shape, BF16),
            vmem(out_weight.shape, BF16),
            pltpu.SemaphoreType.DMA((7,)),
            pltpu.SemaphoreType.DMA((updates, 36)),
            pltpu.SemaphoreType.DMA((updates, 36)),
            vmem((rows, tile, cols), F32),
            vmem((updates, 3, span + 4, 2 * tile, cols), BF16),
            vmem((updates, 3, 3, 2 * tile, cols), BF16),
            vmem((9 * tile, frames * LANES), F32),
            vmem((frames * hidden, 9 * tile), BF16),
            vmem((2, 2 * hidden, 12 * hidden), BF16),
            vmem((2 * chans, 2 * hidden), BF16),
            vmem((3, span, hidden, frames * cols), BF16),
            vmem((3, rows + 2, hidden, frames * cols), BF16),
        ],
        compiler_params=pltpu.CompilerParams(
            collective_id=0, has_side_effects=True, vmem_limit_bytes=60 * 1024 * 1024
        ),
        cost_estimate=pl.CostEstimate(
            flops=4 * updates * tile * rows * cols * hidden * 9 * hidden // chans,
            bytes_accessed=1 << 20,
            transcendentals=0,
        ),
    )(
        step_sizes,
        prior_state.reshape(flat),
        observed.reshape(flat),
        obs_weight.reshape(flat),
        noise_field.reshape(updates, *flat),
        lift_weight.T,
        conv_weights,
        out_weight,
    )
    return result.reshape(prior_state.shape)


def solution(mesh):
    placed = (
        P(("groups", "tm"), None, "lat", "lon"),
        P(("groups", "tm"), None, "lat", "lon"),
        P(("groups", "tm"), None, "lat", "lon"),
        P(None, ("groups", "tm"), None, "lat", "lon"),
        P(),
        P(),
        P(),
        P(),
    )
    return jax.shard_map(
        per_device,
        mesh=mesh,
        in_specs=placed,
        out_specs=P(("groups", "tm"), None, "lat", "lon"),
        check_vma=False,
    )
```

```python
import functools

import jax
import jax.numpy as jnp
from jax import lax
from jax.experimental import pallas as pl
from jax.experimental.pallas import tpu as pltpu
from jax.sharding import PartitionSpec as P

F32 = jnp.float32
BF16 = jnp.bfloat16
LANES = 128


def silu(value):
    half = 0.5 * value
    return half + half * jnp.tanh(half)


def kernel(
    dims,
    steps_ref,
    prior_hbm,
    observed_hbm,
    obs_weight_hbm,
    noise_hbm,
    lift_hbm,
    conv_hbm,
    out_weight_hbm,
    result_ref,
    prior,
    observed,
    obs_weight,
    noise,
    lift_in,
    conv_in,
    out_in,
    load_sem,
    send_sem,
    recv_sem,
    state,
    main,
    edge_in,
    lift_f32,
    lift_w,
    conv_w,
    out_w,
    lifted_cols,
    activated_cols,
):
    frames, chans, rows, cols, hidden, updates, margin = dims
    tile = frames * chans
    group = cols // rows
    span = rows + 2 * margin
    t, t_size = lax.axis_index("tm"), lax.axis_size("tm")
    l, l_size = lax.axis_index("lat"), lax.axis_size("lat")
    other = lax.rem(lax.axis_index("lon") + 1, lax.axis_size("lon"))

    loads = [
        pltpu.make_async_copy(source, target, load_sem.at[index])
        for index, (source, target) in enumerate(
            (
                (prior_hbm, prior),
                (conv_hbm, conv_in),
                (lift_hbm, lift_in),
                (out_weight_hbm, out_in),
                (observed_hbm, observed),
                (obs_weight_hbm, obs_weight),
                (noise_hbm, noise),
            )
        )
    ]
    loads[0].start()
    head = margin + 1
    own_start = head + 1
    own_edge = own_start + rows
    tail = own_edge + 1

    def cleared(ref):
        ref[...] = jnp.zeros(ref.shape, ref.dtype)

    for u in range(updates):
        for slot, absent in ((0, t == 0), (2, t == t_size - 1)):

            @pl.when(absent)
            def _():
                cleared(main.at[u, slot])
                cleared(edge_in.at[u, slot])

        for kind, first, absent in ((0, 0, l == 0), (2, tail, l == l_size - 1)):

            @pl.when(absent)
            def _():
                for slot in range(3):
                    cleared(main.at[u, slot, pl.ds(first, head)])
                    cleared(edge_in.at[u, slot, kind])


    around = [
        (dt, dl, do)
        for dt in (-1, 0, 1)
        for dl in (-1, 0, 1)
        for do in (0, 1)
        if (dt, dl, do) != (0, 0, 0)
    ]

    def exists(dt, dl):
        return (t + dt >= 0) & (t + dt < t_size) & (l + dl >= 0) & (l + dl < l_size)

    def target(dt, dl, do):
        own = lax.axis_index("lon")
        return {"tm": t + dt, "lat": l + dl, "lon": other if do else own}

    barrier = pltpu.get_barrier_semaphore()
    for dt, dl, do in around:

        @pl.when(exists(dt, dl))
        def _():
            pl.semaphore_signal(
                barrier, inc=1, device_id=target(dt, dl, do), device_id_type=pl.DeviceIdType.MESH
            )

    for load in loads[1:]:
        load.start()

    def one(flag):
        return flag.astype(jnp.int32)

    t_count = 1 + one(t > 0) + one(t < t_size - 1)
    l_count = 1 + one(l > 0) + one(l < l_size - 1)

    def message(u, dt, dl, do, chunk=0):
        slot, kind = 1 - dt, 1 - dl
        if do:
            source, place = main.at[u, 1, own_edge], edge_in.at[u, slot, kind]
        else:
            if dl == 1 or (dl == 0 and chunk == 1):
                first, count = own_edge - margin, head
            elif dl == 0:
                first, count = own_start, rows - margin
            else:
                first, count = head, head
            landing = {1: 0, 0: first, -1: tail}[dl]
            source = main.at[u, 1, pl.ds(first, count)]
            place = main.at[u, slot, pl.ds(landing, count)]
        where = ((slot * 3 + kind) * 2 + do) * 2 + chunk
        return pltpu.make_async_remote_copy(
            src_ref=source,
            dst_ref=place,
            send_sem=send_sem.at[u, where],
            recv_sem=recv_sem.at[u, where],
            device_id=target(dt, dl, do),
            device_id_type=pl.DeviceIdType.MESH,
        )

    lane = lax.broadcasted_iota(jnp.int32, (tile, cols), 1)
    lane_group = lane // group
    lane_half = lane % group < group // 2

    def halves(value):
        high = value.astype(BF16)
        return jnp.concatenate([high, (value - high.astype(F32)).astype(BF16)], axis=0)

    def send(u, dt, dl, do, chunk=0):
        @pl.when(exists(dt, dl))
        def _():
            message(u, dt, dl, do, chunk).start()

    def chunks_of(dl, do):
        return range(2) if dl == 0 and not do else range(1)

    def keep(u, row, value):
        state[row] = value
        main[u, 1, own_start + row] = halves(value)

    def send_early(u):
        for dt in (-1, 1):
            send(u, dt, 0, 0, 0)

    def send_edges(u):
        edge = jnp.zeros((tile, cols), F32)
        for row in range(rows):
            value = state[row]
            first = pltpu.roll(value, (group * row + group // 4) % cols, 1)
            last = pltpu.roll(value, (group * row + 3 * group // 4) % cols, 1)
            edge = jnp.where(lane_group == row, jnp.where(lane_half, first, last), edge)
        main[u, 1, head] = halves(edge)
        main[u, 1, own_edge] = halves(edge)
        for dt in (-1, 1):
            send(u, dt, 0, 0, 1)
        for dt in (-1, 1, 0):
            for dl in (-1, 1):
                send(u, dt, dl, 0)
            for dl in (-1, 1, 0):
                send(u, dt, dl, 1)

    def receive_all(u):
        for dt, dl, do in around:

            @pl.when(exists(-dt, -dl))
            def _():
                for chunk in chunks_of(dl, do):
                    message(u, dt, dl, do, chunk).wait_recv()

    def strided(frame, row):
        return pl.ds(frame * chans * rows + row, chans, stride=rows)

    loads[0].wait()
    for row in range(rows):
        keep(
            0,
            row,
            jnp.concatenate([prior[strided(frame, row), :] for frame in range(frames)], axis=0),
        )
    pl.semaphore_wait(barrier, t_count * l_count * 2 - 1)

    send_early(0)
    send_edges(0)

    lift_f32[...] = jnp.zeros_like(lift_f32)
    for load in loads[1:4]:
        load.wait()
    depth = lift_in.shape[0]
    turned = lift_in[...]
    high = turned.astype(BF16).astype(F32)
    low = turned - high
    for frame in range(frames):
        part = pl.ds(frame * LANES, hidden)
        for item in range(depth // chans):
            source = slice(item * chans, (item + 1) * chans)
            slot, place = divmod((item + frame) * chans, tile)
            lift_f32[pl.ds(slot * 2 * tile + place, chans), part] = high[source]
            lift_f32[pl.ds(slot * 2 * tile + tile + place, chans), part] = high[source]
            lift_f32[pl.ds(6 * tile + slot * tile + place, chans), part] = low[source]
    turned = jnp.transpose(lift_f32[...])
    for frame in range(frames):
        lift_w[pl.ds(frame * hidden, hidden)] = turned[
            frame * LANES : frame * LANES + hidden
        ].astype(BF16)
    for layer in range(2):
        taps = [conv_in[layer, tap] for tap in range(9)]
        empty = [jnp.zeros((hidden, hidden), BF16)] * 3
        conv_w[layer, pl.ds(0, hidden)] = jnp.concatenate(taps + empty, axis=1)
        conv_w[layer, pl.ds(hidden, hidden)] = jnp.concatenate(empty + taps, axis=1)
    project = out_in[...].astype(F32)
    blank = jnp.zeros_like(project)
    out_w[...] = jnp.concatenate(
        [jnp.concatenate([project, blank], axis=1), jnp.concatenate([blank, project], axis=1)],
        axis=0,
    ).astype(BF16)
    for load in loads[4:]:
        load.wait()

    lane_tall = lax.broadcasted_iota(jnp.int32, (2 * tile, cols), 1)
    own_lanes = (lane_tall % group >= group // 4) & (lane_tall % group < 3 * group // 4)
    low_lanes = lane_tall < cols // 2
    edge_lane = lax.broadcasted_iota(jnp.int32, (hidden, 2 * cols), 1)

    def shifted(value, edge, row, b):
        first = (group * row + group // 4 - 1) % (2 * cols)
        last = (group * row + 3 * group // 4) % (2 * cols)
        if b == 0:
            return jnp.concatenate([edge[:, first : first + 1], value[:, : cols - 1]], axis=1)
        if b == 2:
            return jnp.concatenate([value[:, 1:], edge[:, last : last + 1]], axis=1)
        return value

    def update(u, carry):
        receive_all(u)

        def rim(slot, kind):
            same = main[u, slot, (margin, own_edge, tail)[kind]]
            return jnp.where(own_lanes, same.astype(F32), edge_in[u, slot, kind].astype(F32))

        tiles = [
            row + (2 if row >= margin else 0) + (2 if row >= margin + rows else 0)
            for row in range(span)
        ]
        blocks = [[main[u, slot, place] for slot in range(3)] for place in tiles]
        blocks.append([rim(slot, 1).astype(BF16) for slot in range(3)])
        blocks.append(
            [jnp.where(low_lanes, rim(slot, 2), rim(slot, 0)).astype(BF16) for slot in range(3)]
        )
        stacked = jnp.concatenate(
            [jnp.concatenate(block + [part[:tile] for part in block], axis=0) for block in blocks],
            axis=1,
        )
        result = jnp.dot(lift_w[...], stacked, preferred_element_type=F32).astype(BF16)
        edges = []
        for frame in range(frames):
            whole = result[frame * hidden : (frame + 1) * hidden]
            part = pl.ds(frame * cols, cols)
            edge = whole[:, span * cols :]
            edges.append(edge)
            for row in range(span):
                value = whole[:, row * cols : (row + 1) * cols]
                for b in range(3):
                    lifted_cols[b, row, :, part] = shifted(value, edge, row - margin, b)

        top = jnp.where(l == 0, 0.0, 1.0).astype(F32)
        bottom = jnp.where(l == l_size - 1, 0.0, 1.0).astype(F32)
        pairs = rows // 2 + 1
        for frame in range(frames):
            turns = []
            for a in range(-1, 2):
                for b in range(-1, 2):
                    turn = (group * a + b) % (2 * cols)
                    edge = edges[frame]
                    if turn:
                        edge = jnp.concatenate([edge[:, turn:], edge[:, :turn]], axis=1)
                    turns.append(edge)
            value = silu(
                jnp.dot(
                    conv_w[0, pl.ds(0, hidden), pl.ds(0, 9 * hidden)],
                    jnp.concatenate(turns, axis=0),
                    preferred_element_type=F32,
                )
            )
            value = jnp.where(edge_lane >= 2 * cols - group, value * top, value)
            after = (edge_lane >= cols) & (edge_lane < cols + group)
            edges[frame] = jnp.where(after, value * bottom, value).astype(BF16)

        for pair in range(pairs):
            window = jnp.concatenate(
                [lifted_cols[b, 2 * pair + r] for r in range(4) for b in range(3)], axis=0
            )
            result = silu(jnp.dot(conv_w[0], window, preferred_element_type=F32))
            for q in range(2):
                value = result[q * hidden : (q + 1) * hidden]
                if pair == 0 and q == 0:
                    value = value * top
                if pair == pairs - 1 and q == 1:
                    value = value * bottom
                value = value.astype(BF16)
                row = 2 * pair + q
                for frame in range(frames):
                    own = value[:, frame * cols : (frame + 1) * cols]
                    for b in range(3):
                        activated_cols[b, row, :, pl.ds(frame * cols, cols)] = shifted(
                            own, edges[frame], row - 1, b
                        )

        step = jnp.full((chans, cols), steps_ref[u], F32)
        spread = jnp.sqrt(2.0 * step)

        for pair in range(rows // 2):
            window = jnp.concatenate(
                [activated_cols[b, 2 * pair + r] for r in range(4) for b in range(3)], axis=0
            )
            second = silu(jnp.dot(conv_w[1], window, preferred_element_type=F32))
            base = jnp.concatenate(
                [lifted_cols[1, margin + 2 * pair + q] for q in range(2)], axis=0
            )
            merged = (base.astype(F32) + second).astype(BF16)
            score = jnp.dot(out_w[...], merged, preferred_element_type=F32)
            for q in range(2):
                row = 2 * pair + q
                fresh = []
                for frame in range(frames):
                    where = strided(frame, row)
                    current = state[row, pl.ds(frame * chans, chans)]
                    drift = score[q * chans : (q + 1) * chans, frame * cols : (frame + 1) * cols]
                    pull = obs_weight[where, :] * (observed[where, :] - current)
                    value = current + step * (drift + pull) + spread * noise[u, where, :]
                    fresh.append(value)
                    result_ref[where, :] = value
                keep(u + 1, row, jnp.concatenate(fresh, axis=0))
            if pair == rows // 2 - 2:

                @pl.when(u < updates - 1)
                def _():
                    send_early(u + 1)

        @pl.when(u < updates - 1)
        def _():
            send_edges(u + 1)

        return carry

    lax.fori_loop(0, updates, update, 0)

    for u in range(updates):
        for dt, dl, do in around:

            @pl.when(exists(dt, dl))
            def _():
                for chunk in chunks_of(dl, do):
                    message(u, dt, dl, do, chunk).wait_send()


def per_device(
    prior_state, observed, obs_weight, noise_field, step_sizes, lift_weight, conv_weights, out_weight
):
    frames, chans, rows, cols = prior_state.shape
    hidden, depth = lift_weight.shape
    updates = noise_field.shape[0]
    margin = 2
    tile = frames * chans
    span = rows + 2 * margin
    flat = (tile * rows, cols)
    dims = (frames, chans, rows, cols, hidden, updates, margin)
    vmem = pltpu.VMEM
    result = pl.pallas_call(
        functools.partial(kernel, dims),
        out_shape=jax.ShapeDtypeStruct(flat, F32),
        in_specs=[pl.BlockSpec(memory_space=pltpu.SMEM)] + [pl.BlockSpec(memory_space=pl.ANY)] * 7,
        out_specs=pl.BlockSpec(memory_space=pltpu.VMEM),
        scratch_shapes=[
            vmem(flat, F32),
            vmem(flat, F32),
            vmem(flat, F32),
            vmem((updates, *flat), F32),
            vmem((depth, hidden), F32),
            vmem(conv_weights.shape, BF16),
            vmem(out_weight.shape, BF16),
            pltpu.SemaphoreType.DMA((7,)),
            pltpu.SemaphoreType.DMA((updates, 36)),
            pltpu.SemaphoreType.DMA((updates, 36)),
            vmem((rows, tile, cols), F32),
            vmem((updates + 1, 3, span + 4, 2 * tile, cols), BF16),
            vmem((updates, 3, 3, 2 * tile, cols), BF16),
            vmem((9 * tile, frames * LANES), F32),
            vmem((frames * hidden, 9 * tile), BF16),
            vmem((2, 2 * hidden, 12 * hidden), BF16),
            vmem((2 * chans, 2 * hidden), BF16),
            vmem((3, span, hidden, frames * cols), BF16),
            vmem((3, rows + 2, hidden, frames * cols), BF16),
        ],
        compiler_params=pltpu.CompilerParams(
            collective_id=0, has_side_effects=True, vmem_limit_bytes=60 * 1024 * 1024
        ),
        cost_estimate=pl.CostEstimate(
            flops=4 * updates * tile * rows * cols * hidden * 9 * hidden // chans,
            bytes_accessed=1 << 20,
            transcendentals=0,
        ),
    )(
        step_sizes,
        prior_state.reshape(flat),
        observed.reshape(flat),
        obs_weight.reshape(flat),
        noise_field.reshape(updates, *flat),
        lift_weight.T,
        conv_weights,
        out_weight,
    )
    return result.reshape(prior_state.shape)


def solution(mesh):
    placed = (
        P(("groups", "tm"), None, "lat", "lon"),
        P(("groups", "tm"), None, "lat", "lon"),
        P(("groups", "tm"), None, "lat", "lon"),
        P(None, ("groups", "tm"), None, "lat", "lon"),
        P(),
        P(),
        P(),
        P(),
    )
    return jax.shard_map(
        per_device,
        mesh=mesh,
        in_specs=placed,
        out_specs=P(("groups", "tm"), None, "lat", "lon"),
        check_vma=False,
    )
```

```python
import functools

import jax
import jax.numpy as jnp
from jax import lax
from jax.experimental import pallas as pl
from jax.experimental.pallas import tpu as pltpu
from jax.sharding import PartitionSpec as P

F32 = jnp.float32
BF16 = jnp.bfloat16
LANES = 128


def silu(value):
    half = 0.5 * value
    return half + half * jnp.tanh(half)


def kernel(
    dims,
    steps_ref,
    prior_hbm,
    observed_hbm,
    obs_weight_hbm,
    noise_hbm,
    lift_hbm,
    conv_hbm,
    out_weight_hbm,
    result_ref,
    prior,
    observed,
    obs_weight,
    noise,
    lift_in,
    conv_in,
    out_in,
    load_sem,
    send_sem,
    recv_sem,
    state,
    main,
    edge_in,
    lift_f32,
    lift_w,
    conv_w,
    out_w,
    lifted_cols,
    activated_cols,
):
    frames, chans, rows, cols, hidden, updates, margin = dims
    tile = frames * chans
    group = cols // rows
    span = rows + 2 * margin
    t, t_size = lax.axis_index("tm"), lax.axis_size("tm")
    l, l_size = lax.axis_index("lat"), lax.axis_size("lat")
    other = lax.rem(lax.axis_index("lon") + 1, lax.axis_size("lon"))

    loads = [
        pltpu.make_async_copy(source, target, load_sem.at[index])
        for index, (source, target) in enumerate(
            (
                (prior_hbm, prior),
                (conv_hbm, conv_in),
                (lift_hbm, lift_in),
                (out_weight_hbm, out_in),
                (observed_hbm, observed),
                (obs_weight_hbm, obs_weight),
                (noise_hbm, noise),
            )
        )
    ]
    loads[0].start()
    head = margin + 1
    own_start = head + 1
    own_edge = own_start + rows
    tail = own_edge + 1

    def cleared(ref):
        ref[...] = jnp.zeros(ref.shape, ref.dtype)

    for u in range(updates):
        for slot, absent in ((0, t == 0), (2, t == t_size - 1)):

            @pl.when(absent)
            def _():
                cleared(main.at[u, slot])
                cleared(edge_in.at[u, slot])

        for kind, first, absent in ((0, 0, l == 0), (2, tail, l == l_size - 1)):

            @pl.when(absent)
            def _():
                for slot in range(3):
                    cleared(main.at[u, slot, pl.ds(first, head)])
                    cleared(edge_in.at[u, slot, kind])


    around = [
        (dt, dl, do)
        for dt in (-1, 0, 1)
        for dl in (-1, 0, 1)
        for do in (0, 1)
        if (dt, dl, do) != (0, 0, 0)
    ]

    def exists(dt, dl):
        return (t + dt >= 0) & (t + dt < t_size) & (l + dl >= 0) & (l + dl < l_size)

    def target(dt, dl, do):
        own = lax.axis_index("lon")
        return {"tm": t + dt, "lat": l + dl, "lon": other if do else own}

    barrier = pltpu.get_barrier_semaphore()
    for dt, dl, do in around:

        @pl.when(exists(dt, dl))
        def _():
            pl.semaphore_signal(
                barrier, inc=1, device_id=target(dt, dl, do), device_id_type=pl.DeviceIdType.MESH
            )

    for load in loads[1:]:
        load.start()

    def one(flag):
        return flag.astype(jnp.int32)

    t_count = 1 + one(t > 0) + one(t < t_size - 1)
    l_count = 1 + one(l > 0) + one(l < l_size - 1)

    def message(u, dt, dl, do, chunk=0):
        slot, kind = 1 - dt, 1 - dl
        if do:
            source, place = main.at[u, 1, own_edge], edge_in.at[u, slot, kind]
        else:
            if dl == 1 or (dl == 0 and chunk == 1):
                first, count = own_edge - margin, head
            elif dl == 0:
                first, count = own_start, rows - margin
            else:
                first, count = head, head
            landing = {1: 0, 0: first, -1: tail}[dl]
            source = main.at[u, 1, pl.ds(first, count)]
            place = main.at[u, slot, pl.ds(landing, count)]
        where = ((slot * 3 + kind) * 2 + do) * 2 + chunk
        return pltpu.make_async_remote_copy(
            src_ref=source,
            dst_ref=place,
            send_sem=send_sem.at[u, where],
            recv_sem=recv_sem.at[u, where],
            device_id=target(dt, dl, do),
            device_id_type=pl.DeviceIdType.MESH,
        )

    lane = lax.broadcasted_iota(jnp.int32, (tile, cols), 1)
    lane_group = lane // group
    lane_half = lane % group < group // 2

    def halves(value):
        high = value.astype(BF16)
        return jnp.concatenate([high, (value - high.astype(F32)).astype(BF16)], axis=0)

    def send(u, dt, dl, do, chunk=0):
        @pl.when(exists(dt, dl))
        def _():
            message(u, dt, dl, do, chunk).start()

    def chunks_of(dl, do):
        return range(2) if dl == 0 and not do else range(1)

    def keep(u, row, value):
        state[row] = value
        main[u, 1, own_start + row] = halves(value)

    def send_early(u):
        for dt in (-1, 1):
            send(u, dt, 0, 0, 0)

    def send_edges(u):
        edge = jnp.zeros((tile, cols), F32)
        for row in range(rows):
            value = state[row]
            first = pltpu.roll(value, (group * row + group // 4) % cols, 1)
            last = pltpu.roll(value, (group * row + 3 * group // 4) % cols, 1)
            edge = jnp.where(lane_group == row, jnp.where(lane_half, first, last), edge)
        main[u, 1, head] = halves(edge)
        main[u, 1, own_edge] = halves(edge)
        for dt in (-1, 1):
            send(u, dt, 0, 0, 1)
        for dt in (-1, 1, 0):
            for dl in (-1, 1):
                send(u, dt, dl, 0)
            for dl in (-1, 1, 0):
                send(u, dt, dl, 1)

    def receive(u, early):
        for dt, dl, do in around:

            @pl.when(exists(-dt, -dl))
            def _():
                for chunk in chunks_of(dl, do):
                    if early == (dl == 0 and not do and chunk == 0):
                        message(u, dt, dl, do, chunk).wait_recv()

    def strided(frame, row):
        return pl.ds(frame * chans * rows + row, chans, stride=rows)

    loads[0].wait()
    for row in range(rows):
        keep(
            0,
            row,
            jnp.concatenate([prior[strided(frame, row), :] for frame in range(frames)], axis=0),
        )
    pl.semaphore_wait(barrier, t_count * l_count * 2 - 1)

    send_early(0)
    send_edges(0)

    lift_f32[...] = jnp.zeros_like(lift_f32)
    for load in loads[1:4]:
        load.wait()
    depth = lift_in.shape[0]
    turned = lift_in[...]
    high = turned.astype(BF16).astype(F32)
    low = turned - high
    for frame in range(frames):
        part = pl.ds(frame * LANES, hidden)
        for item in range(depth // chans):
            source = slice(item * chans, (item + 1) * chans)
            slot, place = divmod((item + frame) * chans, tile)
            lift_f32[pl.ds(slot * 2 * tile + place, chans), part] = high[source]
            lift_f32[pl.ds(slot * 2 * tile + tile + place, chans), part] = high[source]
            lift_f32[pl.ds(6 * tile + slot * tile + place, chans), part] = low[source]
    turned = jnp.transpose(lift_f32[...])
    for frame in range(frames):
        lift_w[pl.ds(frame * hidden, hidden)] = turned[
            frame * LANES : frame * LANES + hidden
        ].astype(BF16)
    for layer in range(2):
        taps = [conv_in[layer, tap] for tap in range(9)]
        empty = [jnp.zeros((hidden, hidden), BF16)] * 3
        conv_w[layer, pl.ds(0, hidden)] = jnp.concatenate(taps + empty, axis=1)
        conv_w[layer, pl.ds(hidden, hidden)] = jnp.concatenate(empty + taps, axis=1)
    project = out_in[...].astype(F32)
    blank = jnp.zeros_like(project)
    out_w[...] = jnp.concatenate(
        [jnp.concatenate([project, blank], axis=1), jnp.concatenate([blank, project], axis=1)],
        axis=0,
    ).astype(BF16)
    for load in loads[4:]:
        load.wait()

    lane_tall = lax.broadcasted_iota(jnp.int32, (2 * tile, cols), 1)
    own_lanes = (lane_tall % group >= group // 4) & (lane_tall % group < 3 * group // 4)
    low_lanes = lane_tall < cols // 2
    edge_lane = lax.broadcasted_iota(jnp.int32, (hidden, 2 * cols), 1)

    def edge_lanes(row):
        first = (group * row + group // 4 - 1) % (2 * cols)
        return first, (group * row + 3 * group // 4) % (2 * cols)

    def shifted(value, edge, row, b):
        first, last = edge_lanes(row)
        if b == 0:
            return jnp.concatenate([edge[:, first : first + 1], value[:, : cols - 1]], axis=1)
        if b == 2:
            return jnp.concatenate([value[:, 1:], edge[:, last : last + 1]], axis=1)
        return value

    def update(u, carry):
        for dt, dl, do in around:

            @pl.when(exists(dt, dl))
            def _():
                for chunk in chunks_of(dl, do):
                    message(u, dt, dl, do, chunk).wait_send()

        receive(u, True)

        def rim(slot, kind):
            same = main[u, slot, (margin, own_edge, tail)[kind]]
            return jnp.where(own_lanes, same.astype(F32), edge_in[u, slot, kind].astype(F32))

        tiles = [
            row + (2 if row >= margin else 0) + (2 if row >= margin + rows else 0)
            for row in range(span)
        ]

        def blocks(row):
            return [main[u, slot, tiles[row]] for slot in range(3)]

        soon = range(margin, rows)
        late = [row for row in range(span) if row not in soon]

        def lift(parts):
            stacked = jnp.concatenate(
                [
                    jnp.concatenate(part + [item[:tile] for item in part], axis=0)
                    for part in parts
                ],
                axis=1,
            )
            return jnp.dot(lift_w[...], stacked, preferred_element_type=F32).astype(BF16)

        result = lift([blocks(row) for row in soon])
        for frame in range(frames):
            part = pl.ds(frame * cols, cols)
            for index, row in enumerate(soon):
                value = result[
                    frame * hidden : (frame + 1) * hidden, index * cols : (index + 1) * cols
                ]
                lifted_cols[1, row, :, part] = value
                lifted_cols[0, row, :, part] = jnp.concatenate(
                    [value[:, cols - 1 :], value[:, : cols - 1]], axis=1
                )
                lifted_cols[2, row, :, part] = jnp.concatenate([value[:, 1:], value[:, :1]], axis=1)

        receive(u, False)
        ends = [rim(slot, 1).astype(BF16) for slot in range(3)]
        far = [jnp.where(low_lanes, rim(slot, 2), rim(slot, 0)).astype(BF16) for slot in range(3)]
        result = lift([blocks(row) for row in late] + [ends, far])
        edges = []
        for frame in range(frames):
            whole = result[frame * hidden : (frame + 1) * hidden]
            part = pl.ds(frame * cols, cols)
            edge = whole[:, len(late) * cols :]
            edges.append(edge)
            for row in soon:
                first, last = edge_lanes(row - margin)
                lifted_cols[0, row, :, part] = jnp.concatenate(
                    [edge[:, first : first + 1], lifted_cols[0, row, :, part][:, 1:]], axis=1
                )
                lifted_cols[2, row, :, part] = jnp.concatenate(
                    [lifted_cols[2, row, :, part][:, : cols - 1], edge[:, last : last + 1]], axis=1
                )
            for index, row in enumerate(late):
                value = whole[:, index * cols : (index + 1) * cols]
                for b in range(3):
                    lifted_cols[b, row, :, part] = shifted(value, edge, row - margin, b)

        top = jnp.where(l == 0, 0.0, 1.0).astype(F32)
        bottom = jnp.where(l == l_size - 1, 0.0, 1.0).astype(F32)
        pairs = rows // 2 + 1
        for frame in range(frames):
            turns = []
            for a in range(-1, 2):
                for b in range(-1, 2):
                    turn = (group * a + b) % (2 * cols)
                    edge = edges[frame]
                    if turn:
                        edge = jnp.concatenate([edge[:, turn:], edge[:, :turn]], axis=1)
                    turns.append(edge)
            value = silu(
                jnp.dot(
                    conv_w[0, pl.ds(0, hidden), pl.ds(0, 9 * hidden)],
                    jnp.concatenate(turns, axis=0),
                    preferred_element_type=F32,
                )
            )
            value = jnp.where(edge_lane >= 2 * cols - group, value * top, value)
            after = (edge_lane >= cols) & (edge_lane < cols + group)
            edges[frame] = jnp.where(after, value * bottom, value).astype(BF16)

        for pair in range(pairs):
            window = jnp.concatenate(
                [lifted_cols[b, 2 * pair + r] for r in range(4) for b in range(3)], axis=0
            )
            result = silu(jnp.dot(conv_w[0], window, preferred_element_type=F32))
            for q in range(2):
                value = result[q * hidden : (q + 1) * hidden]
                if pair == 0 and q == 0:
                    value = value * top
                if pair == pairs - 1 and q == 1:
                    value = value * bottom
                value = value.astype(BF16)
                row = 2 * pair + q
                for frame in range(frames):
                    own = value[:, frame * cols : (frame + 1) * cols]
                    for b in range(3):
                        activated_cols[b, row, :, pl.ds(frame * cols, cols)] = shifted(
                            own, edges[frame], row - 1, b
                        )

        step = jnp.full((chans, cols), steps_ref[u], F32)
        spread = jnp.sqrt(2.0 * step)

        for pair in range(rows // 2):
            window = jnp.concatenate(
                [activated_cols[b, 2 * pair + r] for r in range(4) for b in range(3)], axis=0
            )
            second = silu(jnp.dot(conv_w[1], window, preferred_element_type=F32))
            base = jnp.concatenate(
                [lifted_cols[1, margin + 2 * pair + q] for q in range(2)], axis=0
            )
            merged = (base.astype(F32) + second).astype(BF16)
            score = jnp.dot(out_w[...], merged, preferred_element_type=F32)
            for q in range(2):
                row = 2 * pair + q
                fresh = []
                for frame in range(frames):
                    where = strided(frame, row)
                    current = state[row, pl.ds(frame * chans, chans)]
                    drift = score[q * chans : (q + 1) * chans, frame * cols : (frame + 1) * cols]
                    pull = obs_weight[where, :] * (observed[where, :] - current)
                    value = current + step * (drift + pull) + spread * noise[u, where, :]
                    fresh.append(value)
                    result_ref[where, :] = value
                keep(u + 1, row, jnp.concatenate(fresh, axis=0))
            if pair == rows // 2 - 2:

                @pl.when(u < updates - 1)
                def _():
                    send_early(u + 1)

        @pl.when(u < updates - 1)
        def _():
            send_edges(u + 1)

        return carry

    lax.fori_loop(0, updates, update, 0)


def per_device(
    prior_state, observed, obs_weight, noise_field, step_sizes, lift_weight, conv_weights, out_weight
):
    frames, chans, rows, cols = prior_state.shape
    hidden, depth = lift_weight.shape
    updates = noise_field.shape[0]
    margin = 2
    tile = frames * chans
    span = rows + 2 * margin
    flat = (tile * rows, cols)
    dims = (frames, chans, rows, cols, hidden, updates, margin)
    vmem = pltpu.VMEM
    result = pl.pallas_call(
        functools.partial(kernel, dims),
        out_shape=jax.ShapeDtypeStruct(flat, F32),
        in_specs=[pl.BlockSpec(memory_space=pltpu.SMEM)] + [pl.BlockSpec(memory_space=pl.ANY)] * 7,
        out_specs=pl.BlockSpec(memory_space=pltpu.VMEM),
        scratch_shapes=[
            vmem(flat, F32),
            vmem(flat, F32),
            vmem(flat, F32),
            vmem((updates, *flat), F32),
            vmem((depth, hidden), F32),
            vmem(conv_weights.shape, BF16),
            vmem(out_weight.shape, BF16),
            pltpu.SemaphoreType.DMA((7,)),
            pltpu.SemaphoreType.DMA((updates, 36)),
            pltpu.SemaphoreType.DMA((updates, 36)),
            vmem((rows, tile, cols), F32),
            vmem((updates + 1, 3, span + 4, 2 * tile, cols), BF16),
            vmem((updates, 3, 3, 2 * tile, cols), BF16),
            vmem((9 * tile, frames * LANES), F32),
            vmem((frames * hidden, 9 * tile), BF16),
            vmem((2, 2 * hidden, 12 * hidden), BF16),
            vmem((2 * chans, 2 * hidden), BF16),
            vmem((3, span, hidden, frames * cols), BF16),
            vmem((3, rows + 2, hidden, frames * cols), BF16),
        ],
        compiler_params=pltpu.CompilerParams(
            collective_id=0, has_side_effects=True, vmem_limit_bytes=60 * 1024 * 1024
        ),
        cost_estimate=pl.CostEstimate(
            flops=4 * updates * tile * rows * cols * hidden * 9 * hidden // chans,
            bytes_accessed=1 << 20,
            transcendentals=0,
        ),
    )(
        step_sizes,
        prior_state.reshape(flat),
        observed.reshape(flat),
        obs_weight.reshape(flat),
        noise_field.reshape(updates, *flat),
        lift_weight.T,
        conv_weights,
        out_weight,
    )
    return result.reshape(prior_state.shape)


def solution(mesh):
    placed = (
        P(("groups", "tm"), None, "lat", "lon"),
        P(("groups", "tm"), None, "lat", "lon"),
        P(("groups", "tm"), None, "lat", "lon"),
        P(None, ("groups", "tm"), None, "lat", "lon"),
        P(),
        P(),
        P(),
        P(),
    )
    return jax.shard_map(
        per_device,
        mesh=mesh,
        in_specs=placed,
        out_specs=P(("groups", "tm"), None, "lat", "lon"),
        check_vma=False,
    )
```

```python
import functools

import jax
import jax.numpy as jnp
from jax import lax
from jax.experimental import pallas as pl
from jax.experimental.pallas import tpu as pltpu
from jax.sharding import PartitionSpec as P

F32 = jnp.float32
BF16 = jnp.bfloat16
LANES = 128


def silu(value):
    half = 0.5 * value
    return half + half * jnp.tanh(half)


def kernel(
    dims,
    steps_ref,
    prior_hbm,
    observed_hbm,
    obs_weight_hbm,
    noise_hbm,
    lift_hbm,
    conv_hbm,
    out_weight_hbm,
    result_ref,
    prior,
    observed,
    obs_weight,
    noise,
    lift_in,
    conv_in,
    out_in,
    load_sem,
    send_sem,
    recv_sem,
    state,
    main,
    edge_in,
    lift_f32,
    lift_w,
    conv_w,
    out_w,
    lifted_cols,
    activated_cols,
):
    frames, chans, rows, cols, hidden, updates, margin = dims
    tile = frames * chans
    group = cols // rows
    span = rows + 2 * margin
    t, t_size = lax.axis_index("tm"), lax.axis_size("tm")
    l, l_size = lax.axis_index("lat"), lax.axis_size("lat")
    other = lax.rem(lax.axis_index("lon") + 1, lax.axis_size("lon"))

    loads = [
        pltpu.make_async_copy(source, target, load_sem.at[index])
        for index, (source, target) in enumerate(
            (
                (prior_hbm, prior),
                (conv_hbm, conv_in),
                (lift_hbm, lift_in),
                (out_weight_hbm, out_in),
                (observed_hbm, observed),
                (obs_weight_hbm, obs_weight),
                (noise_hbm, noise),
            )
        )
    ]
    loads[0].start()
    head = margin + 1
    own_start = head + 1
    own_edge = own_start + rows
    tail = own_edge + 1

    def cleared(ref):
        ref[...] = jnp.zeros(ref.shape, ref.dtype)

    for u in range(updates):
        for slot, absent in ((0, t == 0), (2, t == t_size - 1)):

            @pl.when(absent)
            def _():
                cleared(main.at[u, slot])
                cleared(edge_in.at[u, slot])

        for kind, first, absent in ((0, 0, l == 0), (2, tail, l == l_size - 1)):

            @pl.when(absent)
            def _():
                for slot in range(3):
                    cleared(main.at[u, slot, pl.ds(first, head)])
                    cleared(edge_in.at[u, slot, kind])


    around = [
        (dt, dl, do)
        for dt in (-1, 0, 1)
        for dl in (-1, 0, 1)
        for do in (0, 1)
        if (dt, dl, do) != (0, 0, 0)
    ]

    def exists(dt, dl):
        return (t + dt >= 0) & (t + dt < t_size) & (l + dl >= 0) & (l + dl < l_size)

    def target(dt, dl, do):
        own = lax.axis_index("lon")
        return {"tm": t + dt, "lat": l + dl, "lon": other if do else own}

    barrier = pltpu.get_barrier_semaphore()
    for dt, dl, do in around:

        @pl.when(exists(dt, dl))
        def _():
            pl.semaphore_signal(
                barrier, inc=1, device_id=target(dt, dl, do), device_id_type=pl.DeviceIdType.MESH
            )

    for load in loads[1:]:
        load.start()

    def one(flag):
        return flag.astype(jnp.int32)

    t_count = 1 + one(t > 0) + one(t < t_size - 1)
    l_count = 1 + one(l > 0) + one(l < l_size - 1)

    def message(u, dt, dl, do, chunk=0):
        slot, kind = 1 - dt, 1 - dl
        if do:
            source, place = main.at[u, 1, own_edge], edge_in.at[u, slot, kind]
        else:
            if dl == 1 or (dl == 0 and chunk == 1):
                first, count = own_edge - margin, head
            elif dl == 0:
                first, count = own_start, rows - margin
            else:
                first, count = head, head
            landing = {1: 0, 0: first, -1: tail}[dl]
            source = main.at[u, 1, pl.ds(first, count)]
            place = main.at[u, slot, pl.ds(landing, count)]
        where = ((slot * 3 + kind) * 2 + do) * 2 + chunk
        return pltpu.make_async_remote_copy(
            src_ref=source,
            dst_ref=place,
            send_sem=send_sem.at[u, where],
            recv_sem=recv_sem.at[u, where],
            device_id=target(dt, dl, do),
            device_id_type=pl.DeviceIdType.MESH,
        )

    lane = lax.broadcasted_iota(jnp.int32, (tile, cols), 1)
    lane_group = lane // group
    lane_half = lane % group < group // 2

    def halves(value):
        high = value.astype(BF16)
        return jnp.concatenate([high, (value - high.astype(F32)).astype(BF16)], axis=0)

    def send(u, dt, dl, do, chunk=0):
        @pl.when(exists(dt, dl))
        def _():
            message(u, dt, dl, do, chunk).start()

    def chunks_of(dl, do):
        return range(2) if dl == 0 and not do else range(1)

    def keep(u, row, value):
        state[row] = value
        main[u, 1, own_start + row] = halves(value)

    def send_early(u):
        for dt in (-1, 1):
            send(u, dt, 0, 0, 0)

    def send_edges(u):
        edge = jnp.zeros((tile, cols), F32)
        for row in range(rows):
            value = state[row]
            first = pltpu.roll(value, (group * row + group // 4) % cols, 1)
            last = pltpu.roll(value, (group * row + 3 * group // 4) % cols, 1)
            edge = jnp.where(lane_group == row, jnp.where(lane_half, first, last), edge)
        main[u, 1, head] = halves(edge)
        main[u, 1, own_edge] = halves(edge)
        for dt in (-1, 1):
            send(u, dt, 0, 0, 1)
        for dt in (-1, 1, 0):
            for dl in (-1, 1):
                send(u, dt, dl, 0)
            for dl in (-1, 1, 0):
                send(u, dt, dl, 1)

    def receive(u, early):
        for dt, dl, do in around:

            @pl.when(exists(-dt, -dl))
            def _():
                for chunk in chunks_of(dl, do):
                    if early == (dl == 0 and not do and chunk == 0):
                        message(u, dt, dl, do, chunk).wait_recv()

    def strided(frame, row):
        return pl.ds(frame * chans * rows + row, chans, stride=rows)

    loads[0].wait()
    for row in range(rows):
        keep(
            0,
            row,
            jnp.concatenate([prior[strided(frame, row), :] for frame in range(frames)], axis=0),
        )
    pl.semaphore_wait(barrier, t_count * l_count * 2 - 1)

    send_early(0)
    send_edges(0)

    lift_f32[...] = jnp.zeros_like(lift_f32)
    for load in loads[1:4]:
        load.wait()
    depth = lift_in.shape[0]
    turned = lift_in[...]
    high = turned.astype(BF16).astype(F32)
    low = turned - high
    for frame in range(frames):
        part = pl.ds(frame * LANES, hidden)
        for item in range(depth // chans):
            source = slice(item * chans, (item + 1) * chans)
            slot, place = divmod((item + frame) * chans, tile)
            lift_f32[pl.ds(slot * 2 * tile + place, chans), part] = high[source]
            lift_f32[pl.ds(slot * 2 * tile + tile + place, chans), part] = high[source]
            lift_f32[pl.ds(6 * tile + slot * tile + place, chans), part] = low[source]
    turned = jnp.transpose(lift_f32[...])
    for frame in range(frames):
        lift_w[pl.ds(frame * hidden, hidden)] = turned[
            frame * LANES : frame * LANES + hidden
        ].astype(BF16)
    for layer in range(2):
        taps = [conv_in[layer, tap] for tap in range(9)]
        empty = [jnp.zeros((hidden, hidden), BF16)] * 3
        conv_w[layer, pl.ds(0, hidden)] = jnp.concatenate(taps + empty, axis=1)
        conv_w[layer, pl.ds(hidden, hidden)] = jnp.concatenate(empty + taps, axis=1)
    project = out_in[...].astype(F32)
    blank = jnp.zeros_like(project)
    out_w[...] = jnp.concatenate(
        [jnp.concatenate([project, blank], axis=1), jnp.concatenate([blank, project], axis=1)],
        axis=0,
    ).astype(BF16)
    for load in loads[4:]:
        load.wait()

    lane_tall = lax.broadcasted_iota(jnp.int32, (2 * tile, cols), 1)
    own_lanes = (lane_tall % group >= group // 4) & (lane_tall % group < 3 * group // 4)
    low_lanes = lane_tall < cols // 2
    edge_lane = lax.broadcasted_iota(jnp.int32, (hidden, 2 * cols), 1)

    def edge_lanes(row):
        first = (group * row + group // 4 - 1) % (2 * cols)
        return first, (group * row + 3 * group // 4) % (2 * cols)

    def turned_rows(row, part, value):
        lifted_cols[1, row, :, part] = value
        lifted_cols[0, row, :, part] = jnp.concatenate(
            [value[:, cols - 1 :], value[:, : cols - 1]], axis=1
        )
        lifted_cols[2, row, :, part] = jnp.concatenate([value[:, 1:], value[:, :1]], axis=1)

    def shifted(value, edge, row, b):
        first, last = edge_lanes(row)
        inner = value[:, 1 : cols - 1]
        left = edge[:, first : first + 2] if b == 0 else edge[:, first + 1 : first + 2]
        right = edge[:, last - 1 : last + 1] if b == 2 else edge[:, last - 1 : last]
        parts = ([left] if b < 2 else []) + [inner] + ([right] if b > 0 else [])
        return jnp.concatenate(parts, axis=1)

    def first_conv(pair):
        window = jnp.concatenate(
            [lifted_cols[b, 2 * pair + r] for r in range(4) for b in range(3)], axis=0
        )
        return silu(jnp.dot(conv_w[0], window, preferred_element_type=F32))

    def update(u, carry):
        for dt, dl, do in around:

            @pl.when(exists(dt, dl))
            def _():
                for chunk in chunks_of(dl, do):
                    message(u, dt, dl, do, chunk).wait_send()

        receive(u, True)

        def rim(slot, kind):
            same = main[u, slot, (margin, own_edge, tail)[kind]]
            return jnp.where(own_lanes, same.astype(F32), edge_in[u, slot, kind].astype(F32))

        tiles = [
            row + (2 if row >= margin else 0) + (2 if row >= margin + rows else 0)
            for row in range(span)
        ]

        def blocks(row):
            return [main[u, slot, tiles[row]] for slot in range(3)]

        soon = range(margin, rows)
        late = [row for row in range(span) if row not in soon]

        def lift(parts):
            stacked = jnp.concatenate(
                [
                    jnp.concatenate(part + [item[:tile] for item in part], axis=0)
                    for part in parts
                ],
                axis=1,
            )
            return jnp.dot(lift_w[...], stacked, preferred_element_type=F32).astype(BF16)

        result = lift([blocks(row) for row in soon])
        for frame in range(frames):
            part = pl.ds(frame * cols, cols)
            for index, row in enumerate(soon):
                value = result[
                    frame * hidden : (frame + 1) * hidden, index * cols : (index + 1) * cols
                ]
                turned_rows(row, part, value)
        ready = {
            pair: first_conv(pair)
            for pair in range(rows // 2 + 1)
            if 2 * pair in soon and 2 * pair + 3 in soon
        }

        receive(u, False)
        ends = [rim(slot, 1).astype(BF16) for slot in range(3)]
        far = [jnp.where(low_lanes, rim(slot, 2), rim(slot, 0)).astype(BF16) for slot in range(3)]
        result = lift([blocks(row) for row in late] + [ends, far])
        edges = []
        for frame in range(frames):
            whole = result[frame * hidden : (frame + 1) * hidden]
            part = pl.ds(frame * cols, cols)
            edge = whole[:, len(late) * cols :]
            edges.append(edge)
            for index, row in enumerate(late):
                value = whole[:, index * cols : (index + 1) * cols]
                turned_rows(row, part, value)

        top = jnp.where(l == 0, 0.0, 1.0).astype(F32)
        bottom = jnp.where(l == l_size - 1, 0.0, 1.0).astype(F32)
        pairs = rows // 2 + 1
        for frame in range(frames):
            turns = []
            for a in range(-1, 2):
                for b in range(-1, 2):
                    turn = (group * a + b) % (2 * cols)
                    edge = edges[frame]
                    if turn:
                        edge = jnp.concatenate([edge[:, turn:], edge[:, :turn]], axis=1)
                    turns.append(edge)
            value = silu(
                jnp.dot(
                    conv_w[0, pl.ds(0, hidden), pl.ds(0, 9 * hidden)],
                    jnp.concatenate(turns, axis=0),
                    preferred_element_type=F32,
                )
            )
            value = jnp.where(edge_lane >= 2 * cols - group, value * top, value)
            after = (edge_lane >= cols) & (edge_lane < cols + group)
            edges[frame] = jnp.where(after, value * bottom, value).astype(BF16)

        for pair in range(pairs):
            result = ready[pair] if pair in ready else first_conv(pair)
            for q in range(2):
                value = result[q * hidden : (q + 1) * hidden]
                if pair == 0 and q == 0:
                    value = value * top
                if pair == pairs - 1 and q == 1:
                    value = value * bottom
                value = value.astype(BF16)
                row = 2 * pair + q
                for frame in range(frames):
                    own = value[:, frame * cols : (frame + 1) * cols]
                    for b in range(3):
                        activated_cols[b, row, :, pl.ds(frame * cols, cols)] = shifted(
                            own, edges[frame], row - 1, b
                        )

        step = jnp.full((chans, cols), steps_ref[u], F32)
        spread = jnp.sqrt(2.0 * step)

        for pair in range(rows // 2):
            window = jnp.concatenate(
                [activated_cols[b, 2 * pair + r] for r in range(4) for b in range(3)], axis=0
            )
            second = silu(jnp.dot(conv_w[1], window, preferred_element_type=F32))
            base = jnp.concatenate(
                [lifted_cols[1, margin + 2 * pair + q] for q in range(2)], axis=0
            )
            merged = (base.astype(F32) + second).astype(BF16)
            score = jnp.dot(out_w[...], merged, preferred_element_type=F32)
            for q in range(2):
                row = 2 * pair + q
                fresh = []
                for frame in range(frames):
                    where = strided(frame, row)
                    current = state[row, pl.ds(frame * chans, chans)]
                    drift = score[q * chans : (q + 1) * chans, frame * cols : (frame + 1) * cols]
                    pull = obs_weight[where, :] * (observed[where, :] - current)
                    value = current + step * (drift + pull) + spread * noise[u, where, :]
                    fresh.append(value)
                    result_ref[where, :] = value
                keep(u + 1, row, jnp.concatenate(fresh, axis=0))
            if pair == rows // 2 - 2:

                @pl.when(u < updates - 1)
                def _():
                    send_early(u + 1)

        @pl.when(u < updates - 1)
        def _():
            send_edges(u + 1)

        return carry

    lax.fori_loop(0, updates, update, 0)


def per_device(
    prior_state, observed, obs_weight, noise_field, step_sizes, lift_weight, conv_weights, out_weight
):
    frames, chans, rows, cols = prior_state.shape
    hidden, depth = lift_weight.shape
    updates = noise_field.shape[0]
    margin = 2
    tile = frames * chans
    span = rows + 2 * margin
    flat = (tile * rows, cols)
    dims = (frames, chans, rows, cols, hidden, updates, margin)
    vmem = pltpu.VMEM
    result = pl.pallas_call(
        functools.partial(kernel, dims),
        out_shape=jax.ShapeDtypeStruct(flat, F32),
        in_specs=[pl.BlockSpec(memory_space=pltpu.SMEM)] + [pl.BlockSpec(memory_space=pl.ANY)] * 7,
        out_specs=pl.BlockSpec(memory_space=pltpu.VMEM),
        scratch_shapes=[
            vmem(flat, F32),
            vmem(flat, F32),
            vmem(flat, F32),
            vmem((updates, *flat), F32),
            vmem((depth, hidden), F32),
            vmem(conv_weights.shape, BF16),
            vmem(out_weight.shape, BF16),
            pltpu.SemaphoreType.DMA((7,)),
            pltpu.SemaphoreType.DMA((updates, 36)),
            pltpu.SemaphoreType.DMA((updates, 36)),
            vmem((rows, tile, cols), F32),
            vmem((updates + 1, 3, span + 4, 2 * tile, cols), BF16),
            vmem((updates, 3, 3, 2 * tile, cols), BF16),
            vmem((9 * tile, frames * LANES), F32),
            vmem((frames * hidden, 9 * tile), BF16),
            vmem((2, 2 * hidden, 12 * hidden), BF16),
            vmem((2 * chans, 2 * hidden), BF16),
            vmem((3, span, hidden, frames * cols), BF16),
            vmem((3, rows + 2, hidden, frames * cols), BF16),
        ],
        compiler_params=pltpu.CompilerParams(
            collective_id=0, has_side_effects=True, vmem_limit_bytes=60 * 1024 * 1024
        ),
        cost_estimate=pl.CostEstimate(
            flops=4 * updates * tile * rows * cols * hidden * 9 * hidden // chans,
            bytes_accessed=1 << 20,
            transcendentals=0,
        ),
    )(
        step_sizes,
        prior_state.reshape(flat),
        observed.reshape(flat),
        obs_weight.reshape(flat),
        noise_field.reshape(updates, *flat),
        lift_weight.T,
        conv_weights,
        out_weight,
    )
    return result.reshape(prior_state.shape)


def solution(mesh):
    placed = (
        P(("groups", "tm"), None, "lat", "lon"),
        P(("groups", "tm"), None, "lat", "lon"),
        P(("groups", "tm"), None, "lat", "lon"),
        P(None, ("groups", "tm"), None, "lat", "lon"),
        P(),
        P(),
        P(),
        P(),
    )
    return jax.shard_map(
        per_device,
        mesh=mesh,
        in_specs=placed,
        out_specs=P(("groups", "tm"), None, "lat", "lon"),
        check_vma=False,
    )
```
